512 devices in a mesh: lat: 16 (over z_lo, y), lon: 32 (over x, z_hi, core).
Axes of the slice: x: 4, y: 8, z: 8 (z_hi: 4, z_lo: 2; z = z_hi * 2 + z_lo), core: 2. Of those that a mesh axis runs over, the one named last changes fastest.
Arguments:
- queries: bfloat16 [128, 512, 1024], P('lat', 'lon'), may hold values from -8 to 8
- keys: bfloat16 [128, 512, 1024], P('lat', 'lon'), may hold values from -8 to 8
- values: bfloat16 [128, 512, 1024], P('lat', 'lon'), may hold values from -6 to 6
- cotangent: bfloat16 [128, 512, 1024], P('lat', 'lon'), may hold values from -6 to 6
Outputs:
- attended: bfloat16 [128, 512, 1024], P('lat', 'lon')
- query_grad: bfloat16 [128, 512, 1024], P('lat', 'lon')
- key_grad: bfloat16 [128, 512, 1024], P('lat', 'lon')
- value_grad: bfloat16 [128, 512, 1024], P('lat', 'lon')
The draws below stay inside these ranges and needn't reach their ends.
All inputs are finite; a program needn't handle non-finite values.
Results may differ from the reference program's by a relative error of at most 0.009.
Values may be sent and summed in bfloat16 or wider, within the bound.
A program may use at most 64 MiB of HBM per device.

```python
import jax
import jax.numpy as jnp
from jax import lax

H = 16
HD = 64
D = 1024
REACH = 6
SPAN = 13
NLAT = 128
NLON = 512


def draw_queries(key, part):
    key = jax.random.fold_in(key, 11)
    base = jax.random.truncated_normal(key, -8.0, 8.0, (NLAT, NLON, H, HD), jnp.float32)
    return base.reshape(NLAT, NLON, H * HD).astype(jnp.bfloat16)


def draw_keys(key, part):
    key = jax.random.fold_in(key, 12)
    base = jax.random.truncated_normal(key, -8.0, 8.0, (NLAT, NLON, H, HD), jnp.float32)
    return base.reshape(NLAT, NLON, H * HD).astype(jnp.bfloat16)


def block_levels(own_key, extent, shards, smallest, largest):
    def one(dim, blocks):
        draws = jax.random.uniform(jax.random.fold_in(jax.random.fold_in(own_key, 6), dim), (blocks,), jnp.float32, smallest / len(shards), largest / len(shards))
        return jnp.repeat(jnp.exp(draws), extent[dim] // blocks).reshape((-1,) + (1,) * (len(extent) - dim - 1))

    factor_of = one(*shards[0])
    for cut in shards[1:]:
        factor_of = factor_of * one(*cut)
    return factor_of


def normal_values(key, shape, deviation, most, shards=(), held_as=jnp.bfloat16):
    values = deviation * jax.random.normal(key, shape, jnp.float32)
    if shards:
        values = values * block_levels(key, shape, shards, -0.22, 0.18)
    return jnp.clip(values, -most, most).astype(held_as)


def setup_inputs(seed: int = 0) -> dict:
    key_of = jax.random.split(jax.random.key(seed), 5)
    return {
        "queries": draw_queries(jax.random.fold_in(key_of[4], 71), 0),
        "keys": draw_keys(jax.random.fold_in(key_of[4], 71), 0),
        "values": normal_values(key_of[2], (NLAT, NLON, D), 1.0, 6.0, ((0, 16), (1, 32))),
        "cotangent": normal_values(key_of[3], (NLAT, NLON, D), 1.0, 6.0, ((0, 16), (1, 32))),
    }


def pad_grid(field):
    wrapped = jnp.concatenate((field[:, NLON - REACH:], field, field[:, :REACH]), axis=1)
    border = jnp.zeros((REACH,) + wrapped.shape[1:], wrapped.dtype)
    return jnp.concatenate((border, wrapped, border), axis=0)


def cut(padded, row, col):
    zero = jnp.zeros((), jnp.int32)
    starts = (row.astype(jnp.int32), col.astype(jnp.int32)) + (zero,) * (padded.ndim - 2)
    sizes = (NLAT, NLON) + padded.shape[2:]
    return lax.dynamic_slice(padded, starts, sizes)


def as_float(array):
    return array.astype(jnp.float32)


def low_round(array):
    return lax.optimization_barrier(array.astype(jnp.bfloat16)).astype(jnp.float32)


def reference(queries, keys, values, cotangent):
    shape = (NLAT, NLON, H, HD)
    scale = HD ** -0.5
    query_grid = queries.reshape(shape)
    key_grid = keys.reshape(shape)
    value_grid = values.reshape(shape)
    upstream = cotangent.reshape(shape)
    key_pad = pad_grid(key_grid)
    value_pad = pad_grid(value_grid)
    offsets = jnp.arange(SPAN * SPAN, dtype=jnp.int32)
    lat_rows = jnp.arange(NLAT, dtype=jnp.int32)

    def place(offset):
        return (offset // SPAN).astype(jnp.int32), (offset % SPAN).astype(jnp.int32)

    def valid_rows(row):
        lat = lat_rows + row - REACH
        return ((lat >= 0) & (lat < NLAT))[:, None, None]

    def first(carry, offset):
        peak, total = carry
        row, col = place(offset)
        scores = scale * jnp.sum(as_float(query_grid) * as_float(cut(key_pad, row, col)), axis=-1)
        valid = valid_rows(row)
        top = jnp.where(valid, jnp.maximum(peak, scores), peak)
        total = total * jnp.exp(peak - top) + jnp.where(valid, jnp.exp(scores - top), 0.0)
        return (top, total), None

    start_peak = jnp.full((NLAT, NLON, H), -1e30, jnp.float32)
    start_total = jnp.zeros((NLAT, NLON, H), jnp.float32)
    (peak, total), unused = lax.scan(first, (start_peak, start_total), offsets)
    log_total = peak + jnp.log(total)

    def local(offset):
        row, col = place(offset)
        key_win = as_float(cut(key_pad, row, col))
        value_win = as_float(cut(value_pad, row, col))
        scores = scale * jnp.sum(as_float(query_grid) * key_win, axis=-1)
        probs = jnp.where(valid_rows(row), jnp.exp(scores - log_total), 0.0)
        prob_grad = jnp.sum(as_float(upstream) * value_win, axis=-1)
        return key_win, value_win, probs, prob_grad

    def second(carry, offset):
        total_out, delta = carry
        key_win, value_win, probs, prob_grad = local(offset)
        total_out = total_out + low_round(probs)[..., None] * value_win
        delta = delta + probs * prob_grad
        return (total_out, delta), None

    zeros_full = jnp.zeros(shape, jnp.float32)
    (total_out, delta), unused = lax.scan(second, (zeros_full, start_total), offsets)
    attended = total_out.astype(jnp.bfloat16).reshape(NLAT, NLON, H * HD)

    def third(query_acc, offset):
        key_win, value_win, probs, prob_grad = local(offset)
        score_grad = low_round(probs * (prob_grad - delta))
        return query_acc + score_grad[..., None] * key_win, None

    query_acc, unused = lax.scan(third, zeros_full, offsets)
    query_grad = (scale * query_acc).astype(jnp.bfloat16).reshape(NLAT, NLON, H * HD)

    query_pad = pad_grid(query_grid)
    upstream_pad = pad_grid(upstream)
    log_pad = pad_grid(log_total)
    delta_pad = pad_grid(delta)

    def fourth(carry, offset):
        key_acc, value_acc = carry
        row, col = place(offset)
        back_row = (2 * REACH - row).astype(jnp.int32)
        back_col = (2 * REACH - col).astype(jnp.int32)
        query_win = as_float(cut(query_pad, back_row, back_col))
        grad_win = as_float(cut(upstream_pad, back_row, back_col))
        lat = lat_rows + back_row - REACH
        valid = ((lat >= 0) & (lat < NLAT))[:, None, None]
        scores = scale * jnp.sum(as_float(key_grid) * query_win, axis=-1)
        probs = jnp.where(valid, jnp.exp(scores - cut(log_pad, back_row, back_col)), 0.0)
        prob_grad = jnp.sum(as_float(value_grid) * grad_win, axis=-1)
        score_grad = low_round(probs * (prob_grad - cut(delta_pad, back_row, back_col)))
        key_acc = key_acc + score_grad[..., None] * query_win
        value_acc = value_acc + low_round(probs)[..., None] * grad_win
        return (key_acc, value_acc), None

    (key_acc, value_acc), unused = lax.scan(fourth, (zeros_full, zeros_full), offsets)
    key_grad = (scale * key_acc).astype(jnp.bfloat16).reshape(NLAT, NLON, H * HD)
    value_grad = value_acc.astype(jnp.bfloat16).reshape(NLAT, NLON, H * HD)
    return attended, query_grad, key_grad, value_grad
```

```python
import functools

import jax
import jax.numpy as jnp
from jax import lax
from jax.experimental import pallas as pl
from jax.experimental.pallas import tpu as pltpu
from jax.sharding import PartitionSpec as P

HD = 64
REACH = 6
MESH = pl.DeviceIdType.MESH
BF16 = jnp.bfloat16
F32 = jnp.float32

OWN, NORTH, SOUTH, OUTER, OUTER_N, OUTER_S, INNER, SLOTS = 0, 128, 224, 320, 368, 416, 464, 592
HALO = SLOTS - NORTH
GROUPS = 4
NEG = -1e30


def nt(a, b):
    return lax.dot_general(a, b, (((1,), (1,)), ((), ())), preferred_element_type=F32)


def tn(a, b):
    return lax.dot_general(a, b, (((0,), (0,)), ((), ())), preferred_element_type=F32)


def nn(a, b):
    return lax.dot_general(a, b, (((1,), (0,)), ((), ())), preferred_element_type=F32)


def sixth(t):
    return (t * 43) >> 8


def place(slot, outer_col, inner_col):
    far = 1000
    s = slot - OUTER
    six = jnp.where(s < 48, s, jnp.where(s < 96, s - 48, s - 96))
    outer_row = sixth(six)
    outer_row = jnp.where(s < 48, outer_row, jnp.where(s < 96, outer_row - 8, outer_row + 8))
    t = slot - INNER
    u = jnp.where(t < 48, t, jnp.where(t < 84, t - 48, t - 84))
    inner_row = sixth(u)
    inner_row = jnp.where(
        t < 48, inner_row, jnp.where(t < 84, inner_row - REACH, jnp.where(t < 120, inner_row + 8, far))
    )
    wide = slot >> 4
    wide_row = jnp.where(slot < NORTH, wide, jnp.where(slot < SOUTH, wide - 14, wide - 6))
    row = jnp.where(slot < OUTER, wide_row, jnp.where(slot < INNER, outer_row, inner_row))
    col = jnp.where(
        slot < OUTER,
        slot & 15,
        jnp.where(slot < INNER, outer_col + six - 6 * sixth(six), inner_col + u - 6 * sixth(u)),
    )
    return row, col


def kernel(
    lats, lons, k_in, v_in, q_in, g_in, att_out, dq_out, dk_out, dv_out,
    buf, osend, isend, bias1, bias2, own_stat, send_stat, recv_stat, halo_stat,
    att, dq, dk, dv, dk_own, dv_own,
    in_sem, out_sem, lat_s, lat_r, out_s, out_r, cor_s, cor_r, inn_s, inn_r, st_s, st_r,
):
    lat, lon = lax.axis_index("lat"), lax.axis_index("lon")
    core = lax.rem(lon, 2)
    has_n, has_s = lat > 0, lat < lats - 1
    north, south = jnp.maximum(lat - 1, 0), jnp.minimum(lat + 1, lats - 1)
    outer = jnp.where(core == 0, lax.rem(lon + lons - 1, lons), lax.rem(lon + 1, lons))
    inner = jnp.where(core == 0, lon + 1, lon - 1)
    outer_col = jnp.where(core == 0, -REACH, 16)
    inner_col = jnp.where(core == 0, 16, -REACH)
    outer_first = jnp.where(core == 0, 0, 16 - REACH)
    inner_first = jnp.where(core == 0, 16 - REACH, 0)

    loads = [
        pltpu.make_async_copy(x, buf.at[i, OWN:NORTH, :], in_sem.at[i])
        for i, x in enumerate((k_in, v_in, q_in, g_in))
    ]
    for load in loads:
        load.start()

    barrier = pltpu.get_barrier_semaphore()
    for col in (outer, inner):
        pl.semaphore_signal(barrier, inc=1, device_id={"lon": col}, device_id_type=MESH)
    for col in (lon, outer, inner):
        @pl.when(has_n)
        def _():
            pl.semaphore_signal(
                barrier, inc=1, device_id={"lat": north, "lon": col}, device_id_type=MESH
            )

        @pl.when(has_s)
        def _():
            pl.semaphore_signal(
                barrier, inc=1, device_id={"lat": south, "lon": col}, device_id_type=MESH
            )

    @pl.when(jnp.logical_not(has_n))
    def _():
        buf[:, NORTH:SOUTH, :] = jnp.zeros((4, SOUTH - NORTH, 1024), BF16)
        buf[:, OUTER_N:OUTER_S, :] = jnp.zeros((4, 48, 1024), BF16)

    @pl.when(jnp.logical_not(has_s))
    def _():
        buf[:, SOUTH:OUTER, :] = jnp.zeros((4, OUTER - SOUTH, 1024), BF16)
        buf[:, OUTER_S:INNER, :] = jnp.zeros((4, 48, 1024), BF16)

    recv_stat[...] = jnp.zeros(recv_stat.shape, F32)

    pl.semaphore_wait(barrier, 2 + 3 * jnp.where(has_n, 1, 0) + 3 * jnp.where(has_s, 1, 0))

    for load in loads:
        load.wait()

    width = 1024 // GROUPS

    def lanes(g):
        return pl.ds(pl.multiple_of(g * width, width), width)

    def lat_copy(to_north, ph, g):
        src, dst = (OWN, SOUTH) if to_north else (OWN + 32, NORTH)
        d = 0 if to_north else 1
        return pltpu.make_async_remote_copy(
            buf.at[2 * ph : 2 * ph + 2, src : src + 96, lanes(g)],
            buf.at[2 * ph : 2 * ph + 2, dst : dst + 96, lanes(g)],
            lat_s.at[d, ph, g],
            lat_r.at[d, ph, g],
            device_id={"lat": north if to_north else south},
            device_id_type=MESH,
        )

    def corner_copy(to_north, ph, g):
        dst = OUTER_S if to_north else OUTER_N
        d = 0 if to_north else 1
        return pltpu.make_async_remote_copy(
            buf.at[2 * ph : 2 * ph + 2, OUTER : OUTER + 48, lanes(g)],
            buf.at[2 * ph : 2 * ph + 2, dst : dst + 48, lanes(g)],
            cor_s.at[d, ph, g],
            cor_r.at[d, ph, g],
            device_id={"lat": north if to_north else south},
            device_id_type=MESH,
        )

    def outer_copy(ph):
        return pltpu.make_async_remote_copy(
            osend.at[2 * ph : 2 * ph + 2],
            buf.at[2 * ph : 2 * ph + 2, OUTER : OUTER + 48, :],
            out_s.at[ph],
            out_r.at[ph],
            device_id={"lon": outer},
            device_id_type=MESH,
        )

    def inner_copy(ph, g):
        return pltpu.make_async_remote_copy(
            isend.at[2 * ph : 2 * ph + 2, :, lanes(g)],
            buf.at[2 * ph : 2 * ph + 2, INNER:SLOTS, lanes(g)],
            inn_s.at[ph, g],
            inn_r.at[ph, g],
            device_id={"lon": inner},
            device_id_type=MESH,
        )

    def stat_copy(i):
        lat_to, lon_to, part = (
            (north, lon, 0), (south, lon, 1),
            (lat, outer, 2), (north, outer, 2), (south, outer, 2),
            (lat, inner, 3), (north, inner, 4), (south, inner, 5),
        )[i]
        return pltpu.make_async_remote_copy(
            send_stat.at[part],
            recv_stat.at[i],
            st_s.at[i],
            st_r.at[i],
            device_id={"lat": lat_to, "lon": lon_to},
            device_id_type=MESH,
        )

    def each_group(f):
        def step(g, carry):
            f(g)
            return carry

        lax.fori_loop(0, GROUPS, step, 0)

    def start_both(copy, ph):
        @pl.when(has_n)
        def _():
            each_group(lambda g: copy(True, ph, g).start())

        @pl.when(has_s)
        def _():
            each_group(lambda g: copy(False, ph, g).start())

    start_both(lat_copy, 0)

    slot = lax.broadcasted_iota(jnp.int32, (48, 128), 0)
    patch = lax.broadcasted_iota(jnp.int32, (48, 128), 1)
    row6 = sixth(slot)
    at = row6 * 16 + slot - 6 * row6
    pick_outer = jnp.where(patch == at + outer_first, 1.0, 0.0).astype(BF16)
    pick_inner = jnp.where(patch == at + inner_first, 1.0, 0.0).astype(BF16)
    slot = lax.broadcasted_iota(jnp.int32, (80, 192), 0)
    patch = lax.broadcasted_iota(jnp.int32, (80, 192), 1)
    row6 = sixth(slot)
    at = row6 * 16 + slot - 6 * row6
    pick_rim = jnp.where((patch == at + inner_first) & (slot < 72), 1.0, 0.0).astype(BF16)

    for ph in range(2):
        for i in (2 * ph, 2 * ph + 1):
            osend[i] = nn(pick_outer, buf[i, OWN:NORTH, :]).astype(BF16)
        outer_copy(ph).start()
    for i in range(4):
        isend[i, 0:48, :] = nn(pick_inner, buf[i, OWN:NORTH, :]).astype(BF16)

    first_row = lat * 8

    def bias(shape, key_axis, first_key, first_query):
        row_k, col_k = place(
            lax.broadcasted_iota(jnp.int32, shape, key_axis) + first_key, outer_col, inner_col
        )
        row_q, col_q = place(
            lax.broadcasted_iota(jnp.int32, shape, 1 - key_axis) + first_query, outer_col, inner_col
        )
        ok = (jnp.abs(row_k - row_q) <= REACH) & (jnp.abs(col_k - col_q) <= REACH)
        for row in (row_k, row_q):
            ok = ok & (row + first_row >= 0) & (row + first_row < 8 * lats)
        return jnp.where(ok, 0.0, NEG)

    bias1[...] = bias((SLOTS, 128), 0, 0, 0)
    bias2[...] = bias((128, HALO), 0, 0, NORTH)

    outer_copy(0).wait_recv()
    start_both(corner_copy, 0)
    start_both(lat_copy, 1)
    outer_copy(1).wait_recv()
    start_both(corner_copy, 1)

    def rim(ph, g):
        @pl.when(has_s)
        def _():
            lat_copy(True, ph, g).wait_recv()

        @pl.when(has_n)
        def _():
            lat_copy(False, ph, g).wait_recv()

        for i in (2 * ph, 2 * ph + 1):
            isend[i, 48:128, lanes(g)] = nn(pick_rim, buf[i, NORTH:OUTER, lanes(g)]).astype(BF16)
        inner_copy(ph, g).start()

    def arrive(ph, g):
        @pl.when(has_s)
        def _():
            corner_copy(True, ph, g).wait_recv()

        @pl.when(has_n)
        def _():
            corner_copy(False, ph, g).wait_recv()

        inner_copy(ph, g).wait_recv()

    lane = lax.broadcasted_iota(jnp.int32, (128, 128), 1)
    low = jnp.where(lane < HD, 1.0, 0.0).astype(BF16)
    high = jnp.where(lane < HD, 0.0, 1.0).astype(BF16)
    low_f, high_f = low.astype(F32), high.astype(F32)

    def split(x):
        return jnp.concatenate((x * low, x * high), axis=0)

    def joined(x):
        return jnp.concatenate((x[:HD, :128], x[HD:, 128:]), axis=0).T

    def pair_lanes(p):
        return pl.ds(pl.multiple_of(p * 128, 128), 128)

    def first_pass(p):
        at = pair_lanes(p)
        keys, values = buf[0, :, at], buf[1, :, at]
        queries = split(buf[2, OWN:NORTH, at] * jnp.asarray(0.125, BF16))
        upstream = split(buf[3, OWN:NORTH, at])
        near = bias1[...]
        scores = nt(keys, queries) + jnp.concatenate((near, near), axis=1)
        peak = jnp.max(scores, axis=0, keepdims=True)
        e = jnp.exp(scores - peak)
        total = jnp.sum(e, axis=0, keepdims=True)
        probs = e * (1.0 / total)
        prob_grad = nt(values, upstream)
        delta = jnp.sum(probs * prob_grad, axis=0, keepdims=True)
        score_grad = (probs * (prob_grad - delta)).astype(BF16)
        probs_low = probs.astype(BF16)
        att[:, at] = joined(tn(values, probs_low)).astype(BF16)
        dq[:, at] = (joined(tn(keys, score_grad)) * 0.125).astype(BF16)
        dv_own[:, at] = nn(probs_low[OWN:NORTH], upstream)
        dk_own[:, at] = nn(score_grad[OWN:NORTH], queries)
        log_total = peak + jnp.log(total)
        own_stat[pl.ds(2 * p, 1), :] = log_total[:, :128]
        own_stat[pl.ds(2 * p + 1, 1), :] = log_total[:, 128:]
        own_stat[pl.ds(2 * p + 16, 1), :] = delta[:, :128]
        own_stat[pl.ds(2 * p + 17, 1), :] = delta[:, 128:]

    def second_pass(p):
        at = pair_lanes(p)
        keys = split(buf[0, OWN:NORTH, at] * jnp.asarray(0.125, BF16))
        values = split(buf[1, OWN:NORTH, at])
        queries, upstream = buf[2, NORTH:SLOTS, at], buf[3, NORTH:SLOTS, at]
        scores = nt(keys, queries)
        prob_grad = nt(values, upstream)
        near = bias2[...]
        lows, grads = [], []
        for h in range(2):
            here = slice(128 * h, 128 * h + 128)
            probs = jnp.exp(scores[here] + near - halo_stat[pl.ds(2 * p + h, 1), :])
            lows.append(probs.astype(BF16))
            grads.append((probs * (prob_grad[here] - halo_stat[pl.ds(2 * p + 16 + h, 1), :])).astype(BF16))
        value_part = nn(jnp.concatenate(lows, axis=0), upstream)
        key_part = nn(jnp.concatenate(grads, axis=0), queries)
        value_part = value_part[:128] * low_f + value_part[128:] * high_f
        key_part = key_part[:128] * low_f + key_part[128:] * high_f
        dv[:, at] = (dv_own[:, at] + value_part).astype(BF16)
        dk[:, at] = (dk_own[:, at] + key_part * 0.125).astype(BF16)

    def pairs_of(g, f):
        per = 8 // GROUPS

        def step(i, carry):
            f(g * per + i)
            return carry

        lax.fori_loop(0, per, step, 0)

    rim(0, 0)

    def first_group(g):
        @pl.when(g + 1 < GROUPS)
        def _():
            rim(0, g + 1)

        arrive(0, g)
        pairs_of(g, first_pass)

    each_group(first_group)

    s = own_stat[...]
    hi = s.astype(BF16)
    rest = s - hi.astype(F32)
    mid = rest.astype(BF16)
    parts = jnp.concatenate((hi, mid, (rest - mid.astype(F32)).astype(BF16)), axis=0)

    patch = lax.broadcasted_iota(jnp.int32, (128, 128), 0)
    slot = lax.broadcasted_iota(jnp.int32, (128, 128), 1)

    def spread(shift, first, skip_rows, count):
        t = slot - shift
        r = sixth(jnp.maximum(t, 0))
        want = (r + skip_rows) * 16 + t - 6 * r + first
        pick = jnp.where((t >= 0) & (t < count) & (patch == want), 1.0, 0.0).astype(BF16)
        x = nn(parts, pick)
        return x[0:32] + x[32:64] + x[64:96]

    pick = jnp.where(patch == slot + 32, 1.0, 0.0).astype(BF16)
    x = nn(parts, pick)
    send_stat[0] = s
    send_stat[1] = x[0:32] + x[32:64] + x[64:96]
    send_stat[2] = spread(0, outer_first, 0, 48)
    send_stat[3] = spread(0, inner_first, 0, 48)
    send_stat[4] = spread(84, inner_first, 0, 36)
    send_stat[5] = spread(48, inner_first, 2, 36)

    goes = (has_n, has_s, None, has_n, has_s, None, has_n, has_s)
    comes = (has_s, has_n, None, has_s, has_n, None, has_s, has_n)

    def maybe(cond, f):
        if cond is None:
            f()
        else:
            pl.when(cond)(f)

    for i in range(8):
        maybe(goes[i], lambda i=i: stat_copy(i).start())

    stores = [
        pltpu.make_async_copy(att, att_out, out_sem.at[0]),
        pltpu.make_async_copy(dq, dq_out, out_sem.at[1]),
    ]
    for store in stores:
        store.start()

    rim(1, 0)

    for i in range(8):
        maybe(comes[i], lambda i=i: stat_copy(i).wait_recv())
    from_inner = recv_stat[5] + recv_stat[6] + recv_stat[7]
    halo_stat[...] = jnp.concatenate(
        (
            recv_stat[1][:, :96], recv_stat[0][:, :96], recv_stat[2][:, :48],
            recv_stat[4][:, :48], recv_stat[3][:, :48], from_inner,
        ),
        axis=1,
    )

    def second_group(g):
        @pl.when(g + 1 < GROUPS)
        def _():
            rim(1, g + 1)

        arrive(1, g)
        pairs_of(g, second_pass)

    each_group(second_group)

    stores += [
        pltpu.make_async_copy(dk, dk_out, out_sem.at[2]),
        pltpu.make_async_copy(dv, dv_out, out_sem.at[3]),
    ]
    for store in stores[2:]:
        store.start()

    for ph in range(2):
        for copy in (lat_copy, corner_copy):
            @pl.when(has_n)
            def _():
                each_group(lambda g: copy(True, ph, g).wait_send())

            @pl.when(has_s)
            def _():
                each_group(lambda g: copy(False, ph, g).wait_send())

        outer_copy(ph).wait_send()
        each_group(lambda g: inner_copy(ph, g).wait_send())
    for i in range(8):
        maybe(goes[i], lambda i=i: stat_copy(i).wait_send())
    for store in stores:
        store.wait()


def body(lats, lons, queries, keys, values, cotangent):
    flat = [x.reshape(128, 1024) for x in (keys, values, queries, cotangent)]
    dma = pltpu.SemaphoreType.DMA
    outs = pl.pallas_call(
        functools.partial(kernel, lats, lons),
        out_shape=[jax.ShapeDtypeStruct((128, 1024), BF16)] * 4,
        in_specs=[pl.BlockSpec(memory_space=pl.ANY)] * 4,
        out_specs=[pl.BlockSpec(memory_space=pl.ANY)] * 4,
        scratch_shapes=[
            pltpu.VMEM((4, SLOTS, 1024), BF16),
            pltpu.VMEM((4, 48, 1024), BF16),
            pltpu.VMEM((4, 128, 1024), BF16),
            pltpu.VMEM((SLOTS, 128), F32),
            pltpu.VMEM((128, HALO), F32),
            pltpu.VMEM((32, 128), F32),
            pltpu.VMEM((6, 32, 128), F32),
            pltpu.VMEM((8, 32, 128), F32),
            pltpu.VMEM((32, HALO), F32),
            pltpu.VMEM((128, 1024), BF16),
            pltpu.VMEM((128, 1024), BF16),
            pltpu.VMEM((128, 1024), BF16),
            pltpu.VMEM((128, 1024), BF16),
            pltpu.VMEM((128, 1024), F32),
            pltpu.VMEM((128, 1024), F32),
            dma((4,)),
            dma((4,)),
            dma((2, 2, GROUPS)),
            dma((2, 2, GROUPS)),
            dma((2,)),
            dma((2,)),
            dma((2, 2, GROUPS)),
            dma((2, 2, GROUPS)),
            dma((2, GROUPS)),
            dma((2, GROUPS)),
            dma((8,)),
            dma((8,)),
        ],
        compiler_params=pltpu.CompilerParams(
            collective_id=0, has_side_effects=True, vmem_limit_bytes=48 << 20
        ),
    )(*flat)
    return tuple(x.reshape(8, 16, 1024) for x in outs)


def solution(mesh):
    spec = P("lat", "lon", None)
    return jax.shard_map(
        functools.partial(body, mesh.shape["lat"], mesh.shape["lon"]),
        mesh=mesh,
        in_specs=(spec,) * 4,
        out_specs=(spec,) * 4,
        check_vma=False,
    )
```

```python
import functools

import jax
import jax.numpy as jnp
from jax import lax
from jax.experimental import pallas as pl
from jax.experimental.pallas import tpu as pltpu
from jax.sharding import PartitionSpec as P

HD = 64
REACH = 6
MESH = pl.DeviceIdType.MESH
BF16 = jnp.bfloat16
F32 = jnp.float32

OWN, NORTH, SOUTH, OUTER, OUTER_N, OUTER_S, INNER, SLOTS = 0, 128, 224, 320, 368, 416, 464, 592
HALO = SLOTS - NORTH
GROUPS = 4
CHUNK = 208
AHEAD = 2
NEG = -1e30


def nt(a, b):
    return lax.dot_general(a, b, (((1,), (1,)), ((), ())), preferred_element_type=F32)


def tn(a, b):
    return lax.dot_general(a, b, (((0,), (0,)), ((), ())), preferred_element_type=F32)


def nn(a, b):
    return lax.dot_general(a, b, (((1,), (0,)), ((), ())), preferred_element_type=F32)


def sixth(t):
    return (t * 43) >> 8


def place(slot, outer_col, inner_col):
    far = 1000
    s = slot - OUTER
    six = jnp.where(s < 48, s, jnp.where(s < 96, s - 48, s - 96))
    outer_row = sixth(six)
    outer_row = jnp.where(s < 48, outer_row, jnp.where(s < 96, outer_row - 8, outer_row + 8))
    t = slot - INNER
    u = jnp.where(t < 48, t, jnp.where(t < 84, t - 48, t - 84))
    inner_row = sixth(u)
    inner_row = jnp.where(
        t < 48, inner_row, jnp.where(t < 84, inner_row - REACH, jnp.where(t < 120, inner_row + 8, far))
    )
    wide = slot >> 4
    wide_row = jnp.where(slot < NORTH, wide, jnp.where(slot < SOUTH, wide - 14, wide - 6))
    row = jnp.where(slot < OUTER, wide_row, jnp.where(slot < INNER, outer_row, inner_row))
    col = jnp.where(
        slot < OUTER,
        slot & 15,
        jnp.where(slot < INNER, outer_col + six - 6 * sixth(six), inner_col + u - 6 * sixth(u)),
    )
    return row, col


def kernel(
    lats, lons, k_in, v_in, q_in, g_in, outs,
    buf, osend, isend, bias1, bias2, own_stat, send_stat, recv_stat, halo_stat,
    att, dq, dk, dv, dk_own, dv_own, work, work2, low_probs, low_grads,
    ready, in_sem, out_sem, lat_s, lat_r, out_s, out_r, cor_s, cor_r, inn_s, inn_r, st_s, st_r,
):
    lat, lon = lax.axis_index("lat"), lax.axis_index("lon")
    core = lax.rem(lon, 2)
    has_n, has_s = lat > 0, lat < lats - 1
    half = lats // 2
    far_s, far_n = lat == half - 1, lat == half
    first, last = lat == 0, lat == lats - 1
    meets = far_s | far_n | first | last
    north, south = jnp.maximum(lat - 1, 0), jnp.minimum(lat + 1, lats - 1)
    outer = jnp.where(core == 0, lax.rem(lon + lons - 1, lons), lax.rem(lon + 1, lons))
    inner = jnp.where(core == 0, lon + 1, lon - 1)
    turn = lax.rem(lon, 8)
    late = turn == 0
    asks = late | ((core == 1) & (turn < 7))
    outer_col = jnp.where(core == 0, -REACH, 16)
    inner_col = jnp.where(core == 0, 16, -REACH)
    outer_first = jnp.where(core == 0, 0, 16 - REACH)
    inner_first = jnp.where(core == 0, 16 - REACH, 0)

    loads = [
        pltpu.make_async_copy(x, buf.at[i, OWN:NORTH, :], in_sem.at[i])
        for i, x in enumerate((k_in, v_in, q_in, g_in))
    ]
    for load in loads:
        load.start()

    @pl.when(jnp.logical_not(has_n))
    def _():
        buf[:, NORTH:SOUTH, :] = jnp.zeros((4, SOUTH - NORTH, 1024), BF16)
        buf[:, OUTER_N:OUTER_S, :] = jnp.zeros((4, 48, 1024), BF16)

    @pl.when(jnp.logical_not(has_s))
    def _():
        buf[:, SOUTH:OUTER, :] = jnp.zeros((4, OUTER - SOUTH, 1024), BF16)
        buf[:, OUTER_S:INNER, :] = jnp.zeros((4, 48, 1024), BF16)

    recv_stat[...] = jnp.zeros(recv_stat.shape, F32)

    barrier = pltpu.get_barrier_semaphore()
    def greet(sem, col, with_row):
        if with_row:
            pl.semaphore_signal(sem, inc=1, device_id={"lon": col}, device_id_type=MESH)

        @pl.when(has_n)
        def _():
            pl.semaphore_signal(
                sem, inc=1, device_id={"lat": north, "lon": col}, device_id_type=MESH
            )

        @pl.when(has_s)
        def _():
            pl.semaphore_signal(
                sem, inc=1, device_id={"lat": south, "lon": col}, device_id_type=MESH
            )

    greet(barrier, lon, False)
    greet(barrier, inner, True)

    @pl.when(asks)
    def _():
        greet(barrier, outer, True)

    for a in (0, 1):
        to = jnp.where(far_s | far_n, (0, lats - 1)[a], half - 1 + a)

        @pl.when(meets)
        def _():
            pl.semaphore_signal(barrier, inc=1, device_id={"lat": to}, device_id_type=MESH)

    rows = jnp.where(has_n, 1, 0) + jnp.where(has_s, 1, 0)
    pl.semaphore_wait(
        barrier,
        2 * rows + 1 + jnp.where(asks, 0, rows + 1) + 2 * jnp.where(meets, 1, 0),
    )

    @pl.when(jnp.logical_not(asks))
    def _():
        greet(ready, outer, True)

    for load in loads:
        load.wait()

    width = 1024 // GROUPS

    def lanes(g):
        return pl.ds(pl.multiple_of(g * width, width), width)

    def lat_move(sends, recvs, src, dst, ph, g, to_north, lands_north, to):
        rows = 96 if sends is lat_s else 48
        return pltpu.make_async_remote_copy(
            buf.at[2 * ph : 2 * ph + 2, src : src + rows, lanes(g)],
            buf.at[2 * ph : 2 * ph + 2, dst : dst + rows, lanes(g)],
            sends.at[0 if to_north else 1, ph, g],
            recvs.at[1 if lands_north else 0, ph, g],
            device_id={"lat": to},
            device_id_type=MESH,
        )

    def lat_copy(to_north, ph, g, way="direct"):
        own = OWN if to_north else OWN + 32
        above, below = NORTH, SOUTH
        return by_way(lat_s, lat_r, own, above, below, to_north, ph, g, way)

    def corner_copy(to_north, ph, g, way="direct"):
        return by_way(cor_s, cor_r, OUTER, OUTER_N, OUTER_S, to_north, ph, g, way)

    def by_way(sends, recvs, own, above, below, to_north, ph, g, way):
        if way == "direct":
            to = north if to_north else south
            return lat_move(
                sends, recvs, own, below if to_north else above, ph, g, to_north, not to_north, to
            )
        if way == "detour":
            to = 0 if to_north else lats - 1
            return lat_move(
                sends, recvs, own, above if to_north else below, ph, g, to_north, to_north, to
            )
        to = half - 1 if to_north else half
        src, dst = (above, below) if to_north else (below, above)
        return lat_move(sends, recvs, src, dst, ph, g, to_north, not to_north, to)

    def send(copy, to_north, ph, g):
        has = has_n if to_north else has_s
        detour = (far_n if to_north else far_s) & (g % 2 == 1)

        @pl.when(has & jnp.logical_not(detour))
        def _():
            copy(to_north, ph, g).start()

        @pl.when(detour)
        def _():
            copy(to_north, ph, g, "detour").start()

    def wait_sent(copy, to_north, ph, g):
        @pl.when((has_n | (g % 2 == 1)) if to_north else (has_s | (g % 2 == 1)))
        def _():
            copy(to_north, ph, g).wait_send()

    def receive(copy, ph, g):
        @pl.when(has_s)
        def _():
            copy(True, ph, g).wait_recv()

        @pl.when(has_n)
        def _():
            copy(False, ph, g).wait_recv()

    def pass_on(copy, ph, groups=range(1, GROUPS, 2)):
        for g in groups:
            @pl.when(first)
            def _():
                copy(False, ph, g).wait_recv()
                copy(True, ph, g, "onward").start()

            @pl.when(last)
            def _():
                copy(True, ph, g).wait_recv()
                copy(False, ph, g, "onward").start()

    def outer_copy(ph):
        return pltpu.make_async_remote_copy(
            osend.at[2 * ph : 2 * ph + 2],
            buf.at[2 * ph : 2 * ph + 2, OUTER : OUTER + 48, :],
            out_s.at[ph],
            out_r.at[ph],
            device_id={"lon": outer},
            device_id_type=MESH,
        )

    def inner_copy(ph, g):
        return pltpu.make_async_remote_copy(
            isend.at[2 * ph : 2 * ph + 2, :, lanes(g)],
            buf.at[2 * ph : 2 * ph + 2, INNER:SLOTS, lanes(g)],
            inn_s.at[ph, g],
            inn_r.at[ph, g],
            device_id={"lon": inner},
            device_id_type=MESH,
        )

    def stat_copy(i):
        lat_to, lon_to, part = (
            (north, lon, 0), (south, lon, 1),
            (lat, outer, 2), (north, outer, 2), (south, outer, 2),
            (lat, inner, 3), (north, inner, 4), (south, inner, 5),
        )[i]
        return pltpu.make_async_remote_copy(
            send_stat.at[part],
            recv_stat.at[i],
            st_s.at[i],
            st_r.at[i],
            device_id={"lat": lat_to, "lon": lon_to},
            device_id_type=MESH,
        )

    def each_group(f, start=0, stop=GROUPS):
        def step(g, carry):
            f(g)
            return carry

        lax.fori_loop(start, stop, step, 0)

    def start_both(copy, ph, start=0, stop=GROUPS):
        def one(g):
            send(copy, True, ph, g)
            send(copy, False, ph, g)

        each_group(one, start, stop)

    start_both(lat_copy, 0)

    @pl.when(late)
    def _():
        start_both(lat_copy, 1)

    slot = lax.broadcasted_iota(jnp.int32, (48, 128), 0)
    patch = lax.broadcasted_iota(jnp.int32, (48, 128), 1)
    row6 = sixth(slot)
    at = row6 * 16 + slot - 6 * row6
    pick_outer = jnp.where(patch == at + outer_first, 1.0, 0.0).astype(BF16)
    pick_inner = jnp.where(patch == at + inner_first, 1.0, 0.0).astype(BF16)
    slot = lax.broadcasted_iota(jnp.int32, (80, 192), 0)
    patch = lax.broadcasted_iota(jnp.int32, (80, 192), 1)
    row6 = sixth(slot)
    at = row6 * 16 + slot - 6 * row6
    pick_rim = jnp.where((patch == at + inner_first) & (slot < 72), 1.0, 0.0).astype(BF16)

    def rim(ph, g):
        receive(lat_copy, ph, g)
        for i in (2 * ph, 2 * ph + 1):
            isend[i, 48:128, lanes(g)] = nn(pick_rim, buf[i, NORTH:OUTER, lanes(g)]).astype(BF16)
        inner_copy(ph, g).start()

    for i in range(4):
        osend[i] = nn(pick_outer, buf[i, OWN:NORTH, :]).astype(BF16)
        isend[i, 0:48, :] = nn(pick_inner, buf[i, OWN:NORTH, :]).astype(BF16)

    @pl.when(late)
    def _():
        pass_on(lat_copy, 0)
        each_group(lambda g: rim(0, g))

    @pl.when(asks)
    def _():
        pl.semaphore_wait(ready, rows + 1)

    outer_copy(0).start()
    outer_copy(1).start()

    first_row = lat * 8

    def bias(shape, key_axis, first_key, first_query):
        row_k, col_k = place(
            lax.broadcasted_iota(jnp.int32, shape, key_axis) + first_key, outer_col, inner_col
        )
        row_q, col_q = place(
            lax.broadcasted_iota(jnp.int32, shape, 1 - key_axis) + first_query, outer_col, inner_col
        )
        ok = (jnp.abs(row_k - row_q) <= REACH) & (jnp.abs(col_k - col_q) <= REACH)
        for row in (row_k, row_q):
            ok = ok & (row + first_row >= 0) & (row + first_row < 8 * lats)
        return jnp.where(ok, 0.0, NEG)

    bias1[...] = bias((SLOTS, 128), 0, 0, 0)
    bias2[...] = bias((128, HALO), 0, 0, NORTH)

    outer_copy(0).wait_recv()
    start_both(corner_copy, 0)

    @pl.when(jnp.logical_not(late))
    def _():
        start_both(lat_copy, 1, 0, AHEAD)
        pass_on(lat_copy, 0)
        each_group(lambda g: rim(0, g))

    pass_on(corner_copy, 0)


    def arrive(ph, g):
        receive(corner_copy, ph, g)
        inner_copy(ph, g).wait_recv()

    lane = lax.broadcasted_iota(jnp.int32, (128, 128), 1)
    low = jnp.where(lane < HD, 1.0, 0.0).astype(BF16)
    high = jnp.where(lane < HD, 0.0, 1.0).astype(BF16)
    low_f, high_f = low.astype(F32), high.astype(F32)

    def split(x):
        return jnp.concatenate((x * low, x * high), axis=0)

    def joined(x):
        return jnp.concatenate((x[:HD, :128], x[HD:, 128:]), axis=0).T

    def pair_lanes(p):
        return pl.ds(pl.multiple_of(p * 128, 128), 128)

    def first_pass(p):
        at = pair_lanes(p)
        keys, values = buf[0, :, at], buf[1, :, at]
        queries = split(buf[2, OWN:NORTH, at] * jnp.asarray(0.125, BF16))
        upstream = split(buf[3, OWN:NORTH, at])
        cuts = [(r, min(r + CHUNK, SLOTS)) for r in range(0, SLOTS, CHUNK)]
        peak = jnp.full((8, 256), NEG, F32)
        for lo, hi in cuts:
            near = bias1[lo:hi]
            part = nt(keys[lo:hi], queries) + jnp.concatenate((near, near), axis=1)
            work[lo:hi] = part
            peak = jnp.maximum(peak, jnp.max(part.reshape(-1, 8, 256), axis=0))
        peak = jnp.max(peak, axis=0, keepdims=True)
        total = jnp.zeros((8, 256), F32)
        delta = jnp.zeros((8, 256), F32)
        for lo, hi in cuts:
            e = jnp.exp(work[lo:hi] - peak)
            part = nt(values[lo:hi], upstream)
            work[lo:hi] = e
            work2[lo:hi] = part
            total = total + jnp.sum(e.reshape(-1, 8, 256), axis=0)
            delta = delta + jnp.sum((e * part).reshape(-1, 8, 256), axis=0)
        total = jnp.sum(total, axis=0, keepdims=True)
        scale = 1.0 / total
        delta = jnp.sum(delta, axis=0, keepdims=True) * scale
        for lo, hi in cuts:
            probs = work[lo:hi] * scale
            low_probs[lo:hi] = probs.astype(BF16)
            low_grads[lo:hi] = (probs * (work2[lo:hi] - delta)).astype(BF16)
        probs_low, score_grad = low_probs[...], low_grads[...]
        att[:, at] = joined(tn(values, probs_low)).astype(BF16)
        dq[:, at] = (joined(tn(keys, score_grad)) * 0.125).astype(BF16)
        dv_own[:, at] = nn(probs_low[OWN:NORTH], upstream)
        dk_own[:, at] = nn(score_grad[OWN:NORTH], queries)
        log_total = peak + jnp.log(total)
        own_stat[pl.ds(2 * p, 1), :] = log_total[:, :128]
        own_stat[pl.ds(2 * p + 1, 1), :] = log_total[:, 128:]
        own_stat[pl.ds(2 * p + 16, 1), :] = delta[:, :128]
        own_stat[pl.ds(2 * p + 17, 1), :] = delta[:, 128:]

    def second_pass(p):
        at = pair_lanes(p)
        keys = split(buf[0, OWN:NORTH, at] * jnp.asarray(0.125, BF16))
        values = split(buf[1, OWN:NORTH, at])
        queries, upstream = buf[2, NORTH:SLOTS, at], buf[3, NORTH:SLOTS, at]
        scores = nt(keys, queries)
        prob_grad = nt(values, upstream)
        near = bias2[...]
        lows, grads = [], []
        for h in range(2):
            here = slice(128 * h, 128 * h + 128)
            probs = jnp.exp(scores[here] + near - halo_stat[pl.ds(2 * p + h, 1), :])
            lows.append(probs.astype(BF16))
            grads.append((probs * (prob_grad[here] - halo_stat[pl.ds(2 * p + 16 + h, 1), :])).astype(BF16))
        value_part = nn(jnp.concatenate(lows, axis=0), upstream)
        key_part = nn(jnp.concatenate(grads, axis=0), queries)
        value_part = value_part[:128] * low_f + value_part[128:] * high_f
        key_part = key_part[:128] * low_f + key_part[128:] * high_f
        dv[:, at] = (dv_own[:, at] + value_part).astype(BF16)
        dk[:, at] = (dk_own[:, at] + key_part * 0.125).astype(BF16)

    def pairs_of(g, f):
        per = 8 // GROUPS
        for i in range(per):
            f(g * per + i)

    def outer_rest():
        outer_copy(1).wait_recv()
        start_both(corner_copy, 1)

    def first_group(g):
        @pl.when(late & (g == 2))
        def _():
            outer_rest()

        arrive(0, g)
        pairs_of(g, first_pass)

        @pl.when(g == 1)
        def _():
            pass_on(lat_copy, 1, (1,))

    each_group(first_group)

    s = own_stat[...]
    hi = s.astype(BF16)
    rest = s - hi.astype(F32)
    mid = rest.astype(BF16)
    parts = jnp.concatenate((hi, mid, (rest - mid.astype(F32)).astype(BF16)), axis=0)

    patch = lax.broadcasted_iota(jnp.int32, (128, 128), 0)
    slot = lax.broadcasted_iota(jnp.int32, (128, 128), 1)

    def spread(shift, first, skip_rows, count):
        t = slot - shift
        r = sixth(jnp.maximum(t, 0))
        want = (r + skip_rows) * 16 + t - 6 * r + first
        pick = jnp.where((t >= 0) & (t < count) & (patch == want), 1.0, 0.0).astype(BF16)
        x = nn(parts, pick)
        return x[0:32] + x[32:64] + x[64:96]

    pick = jnp.where(patch == slot + 32, 1.0, 0.0).astype(BF16)
    x = nn(parts, pick)
    send_stat[0] = s
    send_stat[1] = x[0:32] + x[32:64] + x[64:96]
    send_stat[2] = spread(0, outer_first, 0, 48)
    send_stat[3] = spread(0, inner_first, 0, 48)
    send_stat[4] = spread(84, inner_first, 0, 36)
    send_stat[5] = spread(48, inner_first, 2, 36)

    goes = (has_n, has_s, None, has_n, has_s, None, has_n, has_s)
    comes = (has_s, has_n, None, has_s, has_n, None, has_s, has_n)

    def maybe(cond, f):
        if cond is None:
            f()
        else:
            pl.when(cond)(f)

    for i in range(8):
        maybe(goes[i], lambda i=i: stat_copy(i).start())

    stores = [
        pltpu.make_async_copy(att, outs.at[0], out_sem.at[0]),
        pltpu.make_async_copy(dq, outs.at[1], out_sem.at[1]),
    ]
    for store in stores:
        store.start()

    @pl.when(jnp.logical_not(late))
    def _():
        start_both(lat_copy, 1, AHEAD, GROUPS)
        outer_rest()

    pass_on(lat_copy, 1, (3,))
    each_group(lambda g: rim(1, g))
    pass_on(corner_copy, 1)

    for i in range(8):
        maybe(comes[i], lambda i=i: stat_copy(i).wait_recv())
    from_inner = recv_stat[5] + recv_stat[6] + recv_stat[7]
    halo_stat[...] = jnp.concatenate(
        (
            recv_stat[1][:, :96], recv_stat[0][:, :96], recv_stat[2][:, :48],
            recv_stat[4][:, :48], recv_stat[3][:, :48], from_inner,
        ),
        axis=1,
    )

    def second_group(g):
        arrive(1, g)
        pairs_of(g, second_pass)

    each_group(second_group)

    stores += [
        pltpu.make_async_copy(dk, outs.at[2], out_sem.at[2]),
        pltpu.make_async_copy(dv, outs.at[3], out_sem.at[3]),
    ]
    for store in stores[2:]:
        store.start()

    for ph in range(2):
        for copy in (lat_copy, corner_copy):
            def sent(g):
                wait_sent(copy, True, ph, g)
                wait_sent(copy, False, ph, g)

            each_group(sent)

        outer_copy(ph).wait_send()
        each_group(lambda g: inner_copy(ph, g).wait_send())
    for i in range(8):
        maybe(goes[i], lambda i=i: stat_copy(i).wait_send())
    for store in stores:
        store.wait()


def body(lats, lons, queries, keys, values, cotangent):
    flat = [
        pltpu.with_memory_space_constraint(x.reshape(128, 1024), pltpu.HBM)
        for x in (keys, values, queries, cotangent)
    ]
    dma = pltpu.SemaphoreType.DMA
    outs = pl.pallas_call(
        functools.partial(kernel, lats, lons),
        out_shape=jax.ShapeDtypeStruct((4, 128, 1024), BF16),
        in_specs=[pl.BlockSpec(memory_space=pltpu.HBM)] * 4,
        out_specs=pl.BlockSpec(memory_space=pl.ANY),
        scratch_shapes=[
            pltpu.VMEM((4, SLOTS, 1024), BF16),
            pltpu.VMEM((4, 48, 1024), BF16),
            pltpu.VMEM((4, 128, 1024), BF16),
            pltpu.VMEM((SLOTS, 128), F32),
            pltpu.VMEM((128, HALO), F32),
            pltpu.VMEM((32, 128), F32),
            pltpu.VMEM((6, 32, 128), F32),
            pltpu.VMEM((8, 32, 128), F32),
            pltpu.VMEM((32, HALO), F32),
            pltpu.VMEM((128, 1024), BF16),
            pltpu.VMEM((128, 1024), BF16),
            pltpu.VMEM((128, 1024), BF16),
            pltpu.VMEM((128, 1024), BF16),
            pltpu.VMEM((128, 1024), F32),
            pltpu.VMEM((128, 1024), F32),
            pltpu.VMEM((SLOTS, 256), F32),
            pltpu.VMEM((SLOTS, 256), F32),
            pltpu.VMEM((SLOTS, 256), BF16),
            pltpu.VMEM((SLOTS, 256), BF16),
            pltpu.SemaphoreType.REGULAR,
            dma((4,)),
            dma((4,)),
            dma((2, 2, GROUPS)),
            dma((2, 2, GROUPS)),
            dma((2,)),
            dma((2,)),
            dma((2, 2, GROUPS)),
            dma((2, 2, GROUPS)),
            dma((2, GROUPS)),
            dma((2, GROUPS)),
            dma((8,)),
            dma((8,)),
        ],
        compiler_params=pltpu.CompilerParams(
            collective_id=0, has_side_effects=True, vmem_limit_bytes=48 << 20
        ),
    )(*flat)
    return tuple(outs[i].reshape(8, 16, 1024) for i in range(4))


def solution(mesh):
    spec = P("lat", "lon", None)
    return jax.shard_map(
        functools.partial(body, mesh.shape["lat"], mesh.shape["lon"]),
        mesh=mesh,
        in_specs=(spec,) * 4,
        out_specs=(spec,) * 4,
        check_vma=False,
    )
```

```python
import functools

import jax
import jax.numpy as jnp
from jax import lax
from jax.experimental import pallas as pl
from jax.experimental.pallas import tpu as pltpu
from jax.sharding import PartitionSpec as P

HD = 64
REACH = 6
MESH = pl.DeviceIdType.MESH
BF16 = jnp.bfloat16
F32 = jnp.float32

OWN, NORTH, SOUTH, OUTER, OUTER_N, OUTER_S, INNER, SLOTS = 0, 128, 224, 320, 368, 416, 464, 592
HALO = SLOTS - NORTH
GROUPS = 4
PER = 2
CHUNK = 208
AHEAD = 2
NEG = -1e30


def nt(a, b):
    return lax.dot_general(a, b, (((1,), (1,)), ((), ())), preferred_element_type=F32)


def tn(a, b):
    return lax.dot_general(a, b, (((0,), (0,)), ((), ())), preferred_element_type=F32)


def nn(a, b):
    return lax.dot_general(a, b, (((1,), (0,)), ((), ())), preferred_element_type=F32)


def sixth(t):
    return (t * 43) >> 8


def place(slot, outer_col, inner_col):
    far = 1000
    s = slot - OUTER
    six = jnp.where(s < 48, s, jnp.where(s < 96, s - 48, s - 96))
    outer_row = sixth(six)
    outer_row = jnp.where(s < 48, outer_row, jnp.where(s < 96, outer_row - 8, outer_row + 8))
    t = slot - INNER
    u = jnp.where(t < 48, t, jnp.where(t < 84, t - 48, t - 84))
    inner_row = sixth(u)
    inner_row = jnp.where(
        t < 48, inner_row, jnp.where(t < 84, inner_row - REACH, jnp.where(t < 120, inner_row + 8, far))
    )
    wide = slot >> 4
    wide_row = jnp.where(slot < NORTH, wide, jnp.where(slot < SOUTH, wide - 14, wide - 6))
    row = jnp.where(slot < OUTER, wide_row, jnp.where(slot < INNER, outer_row, inner_row))
    col = jnp.where(
        slot < OUTER,
        slot & 15,
        jnp.where(slot < INNER, outer_col + six - 6 * sixth(six), inner_col + u - 6 * sixth(u)),
    )
    return row, col


def kernel(
    lats, lons, k_in, v_in, q_in, g_in, outs,
    buf, osend, isend, bias1, bias2, own_stat, send_stat, recv_stat, halo_stat,
    att, dq, dk, dv, dk_own, dv_own, work, work2, low_probs, low_grads,
    picks, ready, in_sem, out_sem, fin_sem, lat_s, lat_r, out_s, out_r, cor_s, cor_r, inn_s, inn_r, st_s, st_r,
):
    lat, lon = lax.axis_index("lat"), lax.axis_index("lon")
    core = lax.rem(lon, 2)
    has_n, has_s = lat > 0, lat < lats - 1
    half = lats // 2
    far_s, far_n = lat == half - 1, lat == half
    first, last = lat == 0, lat == lats - 1
    meets = far_s | far_n | first | last
    north, south = jnp.maximum(lat - 1, 0), jnp.minimum(lat + 1, lats - 1)
    outer = jnp.where(core == 0, lax.rem(lon + lons - 1, lons), lax.rem(lon + 1, lons))
    inner = jnp.where(core == 0, lon + 1, lon - 1)
    turn = lax.rem(lon, 8)
    late = turn == 0
    asks = late | ((core == 1) & (turn < 7))
    outer_col = jnp.where(core == 0, -REACH, 16)
    inner_col = jnp.where(core == 0, 16, -REACH)
    outer_first = jnp.where(core == 0, 0, 16 - REACH)
    inner_first = jnp.where(core == 0, 16 - REACH, 0)

    loads = [
        pltpu.make_async_copy(x, buf.at[i, OWN:NORTH, :], in_sem.at[i])
        for i, x in enumerate((k_in, v_in, q_in, g_in))
    ]
    for load in loads:
        load.start()

    @pl.when(jnp.logical_not(has_n))
    def _():
        buf[:, NORTH:SOUTH, :] = jnp.zeros((4, SOUTH - NORTH, 1024), BF16)
        buf[:, OUTER_N:OUTER_S, :] = jnp.zeros((4, 48, 1024), BF16)

    @pl.when(jnp.logical_not(has_s))
    def _():
        buf[:, SOUTH:OUTER, :] = jnp.zeros((4, OUTER - SOUTH, 1024), BF16)
        buf[:, OUTER_S:INNER, :] = jnp.zeros((4, 48, 1024), BF16)

    recv_stat[...] = jnp.zeros(recv_stat.shape, F32)

    barrier = pltpu.get_barrier_semaphore()
    def greet(sem, col, with_row):
        if with_row:
            pl.semaphore_signal(sem, inc=1, device_id={"lon": col}, device_id_type=MESH)

        @pl.when(has_n)
        def _():
            pl.semaphore_signal(
                sem, inc=1, device_id={"lat": north, "lon": col}, device_id_type=MESH
            )

        @pl.when(has_s)
        def _():
            pl.semaphore_signal(
                sem, inc=1, device_id={"lat": south, "lon": col}, device_id_type=MESH
            )

    greet(barrier, lon, False)
    greet(barrier, inner, True)

    @pl.when(asks)
    def _():
        greet(barrier, outer, True)

    for a in (0, 1):
        to = jnp.where(far_s | far_n, (0, lats - 1)[a], half - 1 + a)

        @pl.when(meets)
        def _():
            pl.semaphore_signal(barrier, inc=1, device_id={"lat": to}, device_id_type=MESH)

    rows = jnp.where(has_n, 1, 0) + jnp.where(has_s, 1, 0)
    pl.semaphore_wait(
        barrier,
        2 * rows + 1 + jnp.where(asks, 0, rows + 1) + 2 * jnp.where(meets, 1, 0),
    )

    @pl.when(jnp.logical_not(asks))
    def _():
        greet(ready, outer, True)

    for load in loads:
        load.wait()

    width = 1024 // GROUPS

    def lanes(g):
        return pl.ds(pl.multiple_of(g * width, width), width)

    def lat_move(sends, recvs, src, dst, ph, g, to_north, lands_north, to):
        rows = 96 if sends is lat_s else 48
        return pltpu.make_async_remote_copy(
            buf.at[2 * ph : 2 * ph + 2, src : src + rows, lanes(g)],
            buf.at[2 * ph : 2 * ph + 2, dst : dst + rows, lanes(g)],
            sends.at[0 if to_north else 1, ph, g],
            recvs.at[1 if lands_north else 0, ph, g],
            device_id={"lat": to},
            device_id_type=MESH,
        )

    def lat_copy(to_north, ph, g, way="direct"):
        own = OWN if to_north else OWN + 32
        above, below = NORTH, SOUTH
        return by_way(lat_s, lat_r, own, above, below, to_north, ph, g, way)

    def corner_copy(to_north, ph, g, way="direct"):
        return by_way(cor_s, cor_r, OUTER, OUTER_N, OUTER_S, to_north, ph, g, way)

    def by_way(sends, recvs, own, above, below, to_north, ph, g, way):
        if way == "direct":
            to = north if to_north else south
            return lat_move(
                sends, recvs, own, below if to_north else above, ph, g, to_north, not to_north, to
            )
        if way == "detour":
            to = 0 if to_north else lats - 1
            return lat_move(
                sends, recvs, own, above if to_north else below, ph, g, to_north, to_north, to
            )
        to = half - 1 if to_north else half
        src, dst = (above, below) if to_north else (below, above)
        return lat_move(sends, recvs, src, dst, ph, g, to_north, not to_north, to)

    def send(copy, to_north, ph, g):
        has = has_n if to_north else has_s
        detour = (far_n if to_north else far_s) & (g % 2 == 1)

        @pl.when(has & jnp.logical_not(detour))
        def _():
            copy(to_north, ph, g).start()

        @pl.when(detour)
        def _():
            copy(to_north, ph, g, "detour").start()

    def wait_sent(copy, to_north, ph, g):
        @pl.when((has_n | (g % 2 == 1)) if to_north else (has_s | (g % 2 == 1)))
        def _():
            copy(to_north, ph, g).wait_send()

    def receive(copy, ph, g):
        @pl.when(has_s)
        def _():
            copy(True, ph, g).wait_recv()

        @pl.when(has_n)
        def _():
            copy(False, ph, g).wait_recv()

    def pass_on(copy, ph, groups=range(1, GROUPS, 2)):
        for g in groups:
            @pl.when(first)
            def _():
                copy(False, ph, g).wait_recv()
                copy(True, ph, g, "onward").start()

            @pl.when(last)
            def _():
                copy(True, ph, g).wait_recv()
                copy(False, ph, g, "onward").start()

    def outer_copy(ph):
        return pltpu.make_async_remote_copy(
            osend.at[2 * ph : 2 * ph + 2],
            buf.at[2 * ph : 2 * ph + 2, OUTER : OUTER + 48, :],
            out_s.at[ph],
            out_r.at[ph],
            device_id={"lon": outer},
            device_id_type=MESH,
        )

    def inner_copy(ph, g):
        return pltpu.make_async_remote_copy(
            isend.at[2 * ph : 2 * ph + 2, :, lanes(g)],
            buf.at[2 * ph : 2 * ph + 2, INNER:SLOTS, lanes(g)],
            inn_s.at[ph, g],
            inn_r.at[ph, g],
            device_id={"lon": inner},
            device_id_type=MESH,
        )

    def stat_copy(i, g):
        lat_to, lon_to, part = (
            (north, lon, 0), (south, lon, 1),
            (lat, outer, 2), (north, outer, 2), (south, outer, 2),
            (lat, inner, 3), (north, inner, 4), (south, inner, 5),
        )[i]
        return pltpu.make_async_remote_copy(
            send_stat.at[g, part],
            recv_stat.at[g, i],
            st_s.at[i, g],
            st_r.at[i, g],
            device_id={"lat": lat_to, "lon": lon_to},
            device_id_type=MESH,
        )

    def each_group(f, start=0, stop=GROUPS):
        def step(g, carry):
            f(g)
            return carry

        lax.fori_loop(start, stop, step, 0)

    def start_both(copy, ph, start=0, stop=GROUPS):
        def one(g):
            send(copy, True, ph, g)
            send(copy, False, ph, g)

        each_group(one, start, stop)

    start_both(lat_copy, 0)

    @pl.when(late)
    def _():
        start_both(lat_copy, 1)

    slot = lax.broadcasted_iota(jnp.int32, (48, 128), 0)
    patch = lax.broadcasted_iota(jnp.int32, (48, 128), 1)
    row6 = sixth(slot)
    at = row6 * 16 + slot - 6 * row6
    pick_outer = jnp.where(patch == at + outer_first, 1.0, 0.0).astype(BF16)
    pick_inner = jnp.where(patch == at + inner_first, 1.0, 0.0).astype(BF16)
    slot = lax.broadcasted_iota(jnp.int32, (80, 192), 0)
    patch = lax.broadcasted_iota(jnp.int32, (80, 192), 1)
    row6 = sixth(slot)
    at = row6 * 16 + slot - 6 * row6
    pick_rim = jnp.where((patch == at + inner_first) & (slot < 72), 1.0, 0.0).astype(BF16)

    def rim(ph, g):
        receive(lat_copy, ph, g)
        for i in (2 * ph, 2 * ph + 1):
            isend[i, 48:128, lanes(g)] = nn(pick_rim, buf[i, NORTH:OUTER, lanes(g)]).astype(BF16)
        inner_copy(ph, g).start()

    for i in range(4):
        osend[i] = nn(pick_outer, buf[i, OWN:NORTH, :]).astype(BF16)
        isend[i, 0:48, :] = nn(pick_inner, buf[i, OWN:NORTH, :]).astype(BF16)

    @pl.when(late)
    def _():
        pass_on(lat_copy, 0)
        each_group(lambda g: rim(0, g))

    @pl.when(asks)
    def _():
        pl.semaphore_wait(ready, rows + 1)

    outer_copy(0).start()
    holds = turn != 7

    @pl.when(jnp.logical_not(holds))
    def _():
        outer_copy(1).start()

    first_row = lat * 8

    def bias(shape, key_axis, first_key, first_query):
        row_k, col_k = place(
            lax.broadcasted_iota(jnp.int32, shape, key_axis) + first_key, outer_col, inner_col
        )
        row_q, col_q = place(
            lax.broadcasted_iota(jnp.int32, shape, 1 - key_axis) + first_query, outer_col, inner_col
        )
        ok = (jnp.abs(row_k - row_q) <= REACH) & (jnp.abs(col_k - col_q) <= REACH)
        for row in (row_k, row_q):
            ok = ok & (row + first_row >= 0) & (row + first_row < 8 * lats)
        return jnp.where(ok, 0.0, NEG)

    bias1[...] = bias((SLOTS, 128), 0, 0, 0)
    bias2[...] = bias((128, HALO), 0, 0, NORTH)

    patch = lax.broadcasted_iota(jnp.int32, (128, 128), 0)
    slot = lax.broadcasted_iota(jnp.int32, (128, 128), 1)

    def spread(shift, edge, skip_rows, count):
        t = slot - shift
        r = sixth(jnp.maximum(t, 0))
        want = (r + skip_rows) * 16 + t - 6 * r + edge
        return jnp.where((t >= 0) & (t < count) & (patch == want), 1.0, 0.0).astype(BF16)

    picks[0] = jnp.where(patch == slot + 32, 1.0, 0.0).astype(BF16)
    picks[1] = spread(0, outer_first, 0, 48)
    picks[2] = spread(0, inner_first, 0, 48)
    picks[3] = spread(84, inner_first, 0, 36)
    picks[4] = spread(48, inner_first, 2, 36)

    goes = (has_n, has_s, None, has_n, has_s, None, has_n, has_s)
    comes = (has_s, has_n, None, has_s, has_n, None, has_s, has_n)

    def maybe(cond, f):
        if cond is None:
            f()
        else:
            pl.when(cond)(f)

    def tell(g):
        s = own_stat[g]
        hi = s.astype(BF16)
        rest = s - hi.astype(F32)
        mid = rest.astype(BF16).astype(F32)
        parts = jnp.concatenate((hi.astype(F32), mid, rest - mid), axis=0).astype(BF16)
        send_stat[g, 0] = s
        for i in range(5):
            x = nn(parts, picks[i])
            send_stat[g, i + 1] = x[0:8] + x[8:16] + x[16:24]
        for i in range(8):
            maybe(goes[i], lambda i=i: stat_copy(i, g).start())

    def hear(g):
        for i in range(8):
            maybe(comes[i], lambda i=i: stat_copy(i, g).wait_recv())
        got = recv_stat[g]
        halo_stat[g] = jnp.concatenate(
            (
                got[1][:, :96], got[0][:, :96], got[2][:, :48], got[4][:, :48], got[3][:, :48],
                got[5] + got[6] + got[7],
            ),
            axis=1,
        )

    outer_copy(0).wait_recv()
    start_both(corner_copy, 0)

    @pl.when(jnp.logical_not(late))
    def _():
        start_both(lat_copy, 1, 0, AHEAD)
        pass_on(lat_copy, 0)
        each_group(lambda g: rim(0, g))

    @pl.when(holds)
    def _():
        outer_copy(1).start()

    pass_on(corner_copy, 0)


    def arrive(ph, g):
        receive(corner_copy, ph, g)
        inner_copy(ph, g).wait_recv()

    lane = lax.broadcasted_iota(jnp.int32, (128, 128), 1)
    low = jnp.where(lane < HD, 1.0, 0.0).astype(BF16)
    high = jnp.where(lane < HD, 0.0, 1.0).astype(BF16)
    low_f, high_f = low.astype(F32), high.astype(F32)

    def split(x):
        return jnp.concatenate((x * low, x * high), axis=0)

    def joined(x):
        return jnp.concatenate((x[:HD, :128], x[HD:, 128:]), axis=0).T

    def pair_lanes(p):
        return pl.ds(pl.multiple_of(p * 128, 128), 128)

    def first_pass(g, i):
        at = pair_lanes(g * PER + i)
        keys, values = buf[0, :, at], buf[1, :, at]
        queries = split(buf[2, OWN:NORTH, at] * jnp.asarray(0.125, BF16))
        upstream = split(buf[3, OWN:NORTH, at])
        cuts = [(r, min(r + CHUNK, SLOTS)) for r in range(0, SLOTS, CHUNK)]
        peak = jnp.full((8, 256), NEG, F32)
        for lo, hi in cuts:
            near = bias1[lo:hi]
            part = nt(keys[lo:hi], queries) + jnp.concatenate((near, near), axis=1)
            work[lo:hi] = part
            peak = jnp.maximum(peak, jnp.max(part.reshape(-1, 8, 256), axis=0))
        peak = jnp.max(peak, axis=0, keepdims=True)
        total = jnp.zeros((8, 256), F32)
        delta = jnp.zeros((8, 256), F32)
        for lo, hi in cuts:
            e = jnp.exp(work[lo:hi] - peak)
            part = nt(values[lo:hi], upstream)
            work[lo:hi] = e
            work2[lo:hi] = part
            total = total + jnp.sum(e.reshape(-1, 8, 256), axis=0)
            delta = delta + jnp.sum((e * part).reshape(-1, 8, 256), axis=0)
        total = jnp.sum(total, axis=0, keepdims=True)
        scale = 1.0 / total
        delta = jnp.sum(delta, axis=0, keepdims=True) * scale
        for lo, hi in cuts:
            probs = work[lo:hi] * scale
            low_probs[lo:hi] = probs.astype(BF16)
            low_grads[lo:hi] = (probs * (work2[lo:hi] - delta)).astype(BF16)
        probs_low, score_grad = low_probs[...], low_grads[...]
        att[:, at] = joined(tn(values, probs_low)).astype(BF16)
        dq[:, at] = (joined(tn(keys, score_grad)) * 0.125).astype(BF16)
        dv_own[:, at] = nn(probs_low[OWN:NORTH], upstream)
        dk_own[:, at] = nn(score_grad[OWN:NORTH], queries)
        log_total = peak + jnp.log(total)
        for h in range(2):
            here = slice(128 * h, 128 * h + 128)
            own_stat[g, 2 * i + h : 2 * i + h + 1, :] = log_total[:, here]
            own_stat[g, 4 + 2 * i + h : 5 + 2 * i + h, :] = delta[:, here]

    def second_pass(g, i):
        at = pair_lanes(g * PER + i)
        keys = split(buf[0, OWN:NORTH, at] * jnp.asarray(0.125, BF16))
        values = split(buf[1, OWN:NORTH, at])
        queries, upstream = buf[2, NORTH:SLOTS, at], buf[3, NORTH:SLOTS, at]
        scores = nt(keys, queries)
        prob_grad = nt(values, upstream)
        near = bias2[...]
        lows, grads = [], []
        for h in range(2):
            here = slice(128 * h, 128 * h + 128)
            probs = jnp.exp(scores[here] + near - halo_stat[g, 2 * i + h : 2 * i + h + 1, :])
            lows.append(probs.astype(BF16))
            change = prob_grad[here] - halo_stat[g, 4 + 2 * i + h : 5 + 2 * i + h, :]
            grads.append((probs * change).astype(BF16))
        value_part = nn(jnp.concatenate(lows, axis=0), upstream)
        key_part = nn(jnp.concatenate(grads, axis=0), queries)
        value_part = value_part[:128] * low_f + value_part[128:] * high_f
        key_part = key_part[:128] * low_f + key_part[128:] * high_f
        dv[:, at] = (dv_own[:, at] + value_part).astype(BF16)
        dk[:, at] = (dk_own[:, at] + key_part * 0.125).astype(BF16)

    def pairs_of(g, f):
        for i in range(PER):
            f(g, i)

    def outer_rest():
        outer_copy(1).wait_recv()
        start_both(corner_copy, 1)

    def first_group(g):
        @pl.when(late & (g == 2))
        def _():
            outer_rest()

        arrive(0, g)
        pairs_of(g, first_pass)
        tell(g)

        @pl.when(jnp.logical_not(late) & (g >= AHEAD - 1) & (g < GROUPS - 1))
        def _():
            send(lat_copy, True, 1, g + 1)
            send(lat_copy, False, 1, g + 1)

        @pl.when(g == 1)
        def _():
            pass_on(lat_copy, 1, (1,))

    each_group(first_group)

    stores = [
        pltpu.make_async_copy(att, outs.at[0], out_sem.at[0]),
        pltpu.make_async_copy(dq, outs.at[1], out_sem.at[1]),
    ]
    for store in stores:
        store.start()

    @pl.when(jnp.logical_not(late))
    def _():
        outer_rest()

    pass_on(lat_copy, 1, (3,))
    each_group(lambda g: rim(1, g))
    pass_on(corner_copy, 1)

    def finals(g):
        return [
            pltpu.make_async_copy(
                x.at[:, lanes(g)], outs.at[2 + i, :, lanes(g)], fin_sem.at[i, g]
            )
            for i, x in enumerate((dk, dv))
        ]

    def second_group(g):
        hear(g)
        arrive(1, g)
        pairs_of(g, second_pass)
        for copy in finals(g):
            copy.start()

    each_group(second_group)

    for ph in range(2):
        for copy in (lat_copy, corner_copy):
            def sent(g):
                wait_sent(copy, True, ph, g)
                wait_sent(copy, False, ph, g)

            each_group(sent)

        outer_copy(ph).wait_send()
        each_group(lambda g: inner_copy(ph, g).wait_send())
    for i in range(8):
        maybe(goes[i], lambda i=i: each_group(lambda g: stat_copy(i, g).wait_send()))
    for store in stores:
        store.wait()

    def ended(g):
        for copy in finals(g):
            copy.wait()

    each_group(ended)


def body(lats, lons, queries, keys, values, cotangent):
    flat = [
        pltpu.with_memory_space_constraint(x.reshape(128, 1024), pltpu.HBM)
        for x in (keys, values, queries, cotangent)
    ]
    dma = pltpu.SemaphoreType.DMA
    outs = pl.pallas_call(
        functools.partial(kernel, lats, lons),
        out_shape=jax.ShapeDtypeStruct((4, 128, 1024), BF16),
        in_specs=[pl.BlockSpec(memory_space=pltpu.HBM)] * 4,
        out_specs=pl.BlockSpec(memory_space=pl.ANY),
        scratch_shapes=[
            pltpu.VMEM((4, SLOTS, 1024), BF16),
            pltpu.VMEM((4, 48, 1024), BF16),
            pltpu.VMEM((4, 128, 1024), BF16),
            pltpu.VMEM((SLOTS, 128), F32),
            pltpu.VMEM((128, HALO), F32),
            pltpu.VMEM((GROUPS, 8, 128), F32),
            pltpu.VMEM((GROUPS, 6, 8, 128), F32),
            pltpu.VMEM((GROUPS, 8, 8, 128), F32),
            pltpu.VMEM((GROUPS, 8, HALO), F32),
            pltpu.VMEM((128, 1024), BF16),
            pltpu.VMEM((128, 1024), BF16),
            pltpu.VMEM((128, 1024), BF16),
            pltpu.VMEM((128, 1024), BF16),
            pltpu.VMEM((128, 1024), F32),
            pltpu.VMEM((128, 1024), F32),
            pltpu.VMEM((SLOTS, 256), F32),
            pltpu.VMEM((SLOTS, 256), F32),
            pltpu.VMEM((SLOTS, 256), BF16),
            pltpu.VMEM((SLOTS, 256), BF16),
            pltpu.VMEM((5, 128, 128), BF16),
            pltpu.SemaphoreType.REGULAR,
            dma((4,)),
            dma((2,)),
            dma((2, GROUPS)),
            dma((2, 2, GROUPS)),
            dma((2, 2, GROUPS)),
            dma((2,)),
            dma((2,)),
            dma((2, 2, GROUPS)),
            dma((2, 2, GROUPS)),
            dma((2, GROUPS)),
            dma((2, GROUPS)),
            dma((8, GROUPS)),
            dma((8, GROUPS)),
        ],
        compiler_params=pltpu.CompilerParams(
            collective_id=0, has_side_effects=True, vmem_limit_bytes=48 << 20
        ),
    )(*flat)
    return tuple(outs[i].reshape(8, 16, 1024) for i in range(4))


def solution(mesh):
    spec = P("lat", "lon", None)
    return jax.shard_map(
        functools.partial(body, mesh.shape["lat"], mesh.shape["lon"]),
        mesh=mesh,
        in_specs=(spec,) * 4,
        out_specs=(spec,) * 4,
        check_vma=False,
    )
```

```python
import functools

import jax
import jax.numpy as jnp
from jax import lax
from jax.experimental import pallas as pl
from jax.experimental.pallas import tpu as pltpu
from jax.sharding import PartitionSpec as P

HD = 64
REACH = 6
MESH = pl.DeviceIdType.MESH
BF16 = jnp.bfloat16
F32 = jnp.float32

OWN, NORTH, SOUTH, OUTER, OUTER_N, OUTER_S, INNER, SLOTS = 0, 128, 224, 320, 368, 416, 464, 592
HALO = SLOTS - NORTH
GROUPS = 4
PER = 2
TOLD = 2
CHUNK = 208
AHEAD = 2
NEG = -1e30


def nt(a, b):
    return lax.dot_general(a, b, (((1,), (1,)), ((), ())), preferred_element_type=F32)


def tn(a, b):
    return lax.dot_general(a, b, (((0,), (0,)), ((), ())), preferred_element_type=F32)


def nn(a, b):
    return lax.dot_general(a, b, (((1,), (0,)), ((), ())), preferred_element_type=F32)


def sixth(t):
    return (t * 43) >> 8


def place(slot, outer_col, inner_col):
    far = 1000
    s = slot - OUTER
    six = jnp.where(s < 48, s, jnp.where(s < 96, s - 48, s - 96))
    outer_row = sixth(six)
    outer_row = jnp.where(s < 48, outer_row, jnp.where(s < 96, outer_row - 8, outer_row + 8))
    t = slot - INNER
    u = jnp.where(t < 48, t, jnp.where(t < 84, t - 48, t - 84))
    inner_row = sixth(u)
    inner_row = jnp.where(
        t < 48, inner_row, jnp.where(t < 84, inner_row - REACH, jnp.where(t < 120, inner_row + 8, far))
    )
    wide = slot >> 4
    wide_row = jnp.where(slot < NORTH, wide, jnp.where(slot < SOUTH, wide - 14, wide - 6))
    row = jnp.where(slot < OUTER, wide_row, jnp.where(slot < INNER, outer_row, inner_row))
    col = jnp.where(
        slot < OUTER,
        slot & 15,
        jnp.where(slot < INNER, outer_col + six - 6 * sixth(six), inner_col + u - 6 * sixth(u)),
    )
    return row, col


def kernel(
    lats, lons, k_in, v_in, q_in, g_in, outs,
    buf, osend, isend, bias1, bias2, own_stat, send_stat, recv_stat, halo_stat,
    att, dq, dk, dv, dk_own, dv_own, work, work2, low_probs, low_grads,
    picks, ready, in_sem, out_sem, fin_sem, lat_s, lat_r, out_s, out_r, cor_s, cor_r, inn_s, inn_r, st_s, st_r,
):
    lat, lon = lax.axis_index("lat"), lax.axis_index("lon")
    core = lax.rem(lon, 2)
    has_n, has_s = lat > 0, lat < lats - 1
    half = lats // 2
    far_s, far_n = lat == half - 1, lat == half
    first, last = lat == 0, lat == lats - 1
    meets = far_s | far_n | first | last
    north, south = jnp.maximum(lat - 1, 0), jnp.minimum(lat + 1, lats - 1)
    outer = jnp.where(core == 0, lax.rem(lon + lons - 1, lons), lax.rem(lon + 1, lons))
    inner = jnp.where(core == 0, lon + 1, lon - 1)
    turn = lax.rem(lon, 8)
    late = turn == 0
    asks = late | ((core == 1) & (turn < 7))
    outer_col = jnp.where(core == 0, -REACH, 16)
    inner_col = jnp.where(core == 0, 16, -REACH)
    outer_first = jnp.where(core == 0, 0, 16 - REACH)
    inner_first = jnp.where(core == 0, 16 - REACH, 0)

    loads = [
        pltpu.make_async_copy(x, buf.at[i, OWN:NORTH, :], in_sem.at[i])
        for i, x in enumerate((k_in, v_in, q_in, g_in))
    ]
    for load in loads:
        load.start()

    @pl.when(jnp.logical_not(has_n))
    def _():
        buf[:, NORTH:SOUTH, :] = jnp.zeros((4, SOUTH - NORTH, 1024), BF16)
        buf[:, OUTER_N:OUTER_S, :] = jnp.zeros((4, 48, 1024), BF16)

    @pl.when(jnp.logical_not(has_s))
    def _():
        buf[:, SOUTH:OUTER, :] = jnp.zeros((4, OUTER - SOUTH, 1024), BF16)
        buf[:, OUTER_S:INNER, :] = jnp.zeros((4, 48, 1024), BF16)

    recv_stat[...] = jnp.zeros(recv_stat.shape, F32)

    barrier = pltpu.get_barrier_semaphore()
    def greet(sem, col, with_row):
        if with_row:
            pl.semaphore_signal(sem, inc=1, device_id={"lon": col}, device_id_type=MESH)

        @pl.when(has_n)
        def _():
            pl.semaphore_signal(
                sem, inc=1, device_id={"lat": north, "lon": col}, device_id_type=MESH
            )

        @pl.when(has_s)
        def _():
            pl.semaphore_signal(
                sem, inc=1, device_id={"lat": south, "lon": col}, device_id_type=MESH
            )

    greet(barrier, lon, False)
    greet(barrier, inner, True)

    @pl.when(asks)
    def _():
        greet(barrier, outer, True)

    for a in (0, 1):
        to = jnp.where(far_s | far_n, (0, lats - 1)[a], half - 1 + a)

        @pl.when(meets)
        def _():
            pl.semaphore_signal(barrier, inc=1, device_id={"lat": to}, device_id_type=MESH)

    rows = jnp.where(has_n, 1, 0) + jnp.where(has_s, 1, 0)
    pl.semaphore_wait(
        barrier,
        2 * rows + 1 + jnp.where(asks, 0, rows + 1) + 2 * jnp.where(meets, 1, 0),
    )

    @pl.when(jnp.logical_not(asks))
    def _():
        greet(ready, outer, True)

    for load in loads:
        load.wait()

    width = 1024 // GROUPS

    def lanes(g):
        return pl.ds(pl.multiple_of(g * width, width), width)

    def lat_move(sends, recvs, src, dst, ph, g, to_north, lands_north, to):
        rows = 96 if sends is lat_s else 48
        return pltpu.make_async_remote_copy(
            buf.at[2 * ph : 2 * ph + 2, src : src + rows, lanes(g)],
            buf.at[2 * ph : 2 * ph + 2, dst : dst + rows, lanes(g)],
            sends.at[0 if to_north else 1, ph, g],
            recvs.at[1 if lands_north else 0, ph, g],
            device_id={"lat": to},
            device_id_type=MESH,
        )

    def lat_copy(to_north, ph, g, way="direct"):
        own = OWN if to_north else OWN + 32
        above, below = NORTH, SOUTH
        return by_way(lat_s, lat_r, own, above, below, to_north, ph, g, way)

    def corner_copy(to_north, ph, g, way="direct"):
        return by_way(cor_s, cor_r, OUTER, OUTER_N, OUTER_S, to_north, ph, g, way)

    def by_way(sends, recvs, own, above, below, to_north, ph, g, way):
        if way == "direct":
            to = north if to_north else south
            return lat_move(
                sends, recvs, own, below if to_north else above, ph, g, to_north, not to_north, to
            )
        if way == "detour":
            to = 0 if to_north else lats - 1
            return lat_move(
                sends, recvs, own, above if to_north else below, ph, g, to_north, to_north, to
            )
        to = half - 1 if to_north else half
        src, dst = (above, below) if to_north else (below, above)
        return lat_move(sends, recvs, src, dst, ph, g, to_north, not to_north, to)

    def send(copy, to_north, ph, g):
        has = has_n if to_north else has_s
        detour = (far_n if to_north else far_s) & (g % 2 == 1)

        @pl.when(has & jnp.logical_not(detour))
        def _():
            copy(to_north, ph, g).start()

        @pl.when(detour)
        def _():
            copy(to_north, ph, g, "detour").start()

    def wait_sent(copy, to_north, ph, g):
        @pl.when((has_n | (g % 2 == 1)) if to_north else (has_s | (g % 2 == 1)))
        def _():
            copy(to_north, ph, g).wait_send()

    def receive(copy, ph, g):
        @pl.when(has_s)
        def _():
            copy(True, ph, g).wait_recv()

        @pl.when(has_n)
        def _():
            copy(False, ph, g).wait_recv()

    def pass_on(copy, ph, groups=range(1, GROUPS, 2)):
        for g in groups:
            @pl.when(first)
            def _():
                copy(False, ph, g).wait_recv()
                copy(True, ph, g, "onward").start()

            @pl.when(last)
            def _():
                copy(True, ph, g).wait_recv()
                copy(False, ph, g, "onward").start()

    def outer_copy(ph):
        return pltpu.make_async_remote_copy(
            osend.at[2 * ph : 2 * ph + 2],
            buf.at[2 * ph : 2 * ph + 2, OUTER : OUTER + 48, :],
            out_s.at[ph],
            out_r.at[ph],
            device_id={"lon": outer},
            device_id_type=MESH,
        )

    def inner_copy(ph, g):
        return pltpu.make_async_remote_copy(
            isend.at[2 * ph : 2 * ph + 2, :, lanes(g)],
            buf.at[2 * ph : 2 * ph + 2, INNER:SLOTS, lanes(g)],
            inn_s.at[ph, g],
            inn_r.at[ph, g],
            device_id={"lon": inner},
            device_id_type=MESH,
        )

    def stat_copy(i, g):
        lat_to, lon_to, part = (
            (north, lon, 0), (south, lon, 1),
            (lat, outer, 2), (north, outer, 2), (south, outer, 2),
            (lat, inner, 3), (north, inner, 4), (south, inner, 5),
        )[i]
        return pltpu.make_async_remote_copy(
            send_stat.at[g, part],
            recv_stat.at[g, i],
            st_s.at[i, g],
            st_r.at[i, g],
            device_id={"lat": lat_to, "lon": lon_to},
            device_id_type=MESH,
        )

    def each_group(f, start=0, stop=GROUPS):
        def step(g, carry):
            f(g)
            return carry

        lax.fori_loop(start, stop, step, 0)

    def start_both(copy, ph, start=0, stop=GROUPS):
        def one(g):
            send(copy, True, ph, g)
            send(copy, False, ph, g)

        each_group(one, start, stop)

    start_both(lat_copy, 0)

    @pl.when(late)
    def _():
        start_both(lat_copy, 1)

    slot = lax.broadcasted_iota(jnp.int32, (48, 128), 0)
    patch = lax.broadcasted_iota(jnp.int32, (48, 128), 1)
    row6 = sixth(slot)
    at = row6 * 16 + slot - 6 * row6
    pick_outer = jnp.where(patch == at + outer_first, 1.0, 0.0).astype(BF16)
    pick_inner = jnp.where(patch == at + inner_first, 1.0, 0.0).astype(BF16)
    slot = lax.broadcasted_iota(jnp.int32, (80, 192), 0)
    patch = lax.broadcasted_iota(jnp.int32, (80, 192), 1)
    row6 = sixth(slot)
    at = row6 * 16 + slot - 6 * row6
    pick_rim = jnp.where((patch == at + inner_first) & (slot < 72), 1.0, 0.0).astype(BF16)

    def rim(ph, g):
        receive(lat_copy, ph, g)
        for i in (2 * ph, 2 * ph + 1):
            isend[i, 48:128, lanes(g)] = nn(pick_rim, buf[i, NORTH:OUTER, lanes(g)]).astype(BF16)
        inner_copy(ph, g).start()

    for i in range(4):
        osend[i] = nn(pick_outer, buf[i, OWN:NORTH, :]).astype(BF16)
        isend[i, 0:48, :] = nn(pick_inner, buf[i, OWN:NORTH, :]).astype(BF16)

    @pl.when(late)
    def _():
        pass_on(lat_copy, 0)
        each_group(lambda g: rim(0, g))

    @pl.when(asks)
    def _():
        pl.semaphore_wait(ready, rows + 1)

    outer_copy(0).start()
    holds = turn != 7

    @pl.when(jnp.logical_not(holds))
    def _():
        outer_copy(1).start()

    first_row = lat * 8

    def bias(shape, key_axis, first_key, first_query):
        row_k, col_k = place(
            lax.broadcasted_iota(jnp.int32, shape, key_axis) + first_key, outer_col, inner_col
        )
        row_q, col_q = place(
            lax.broadcasted_iota(jnp.int32, shape, 1 - key_axis) + first_query, outer_col, inner_col
        )
        ok = (jnp.abs(row_k - row_q) <= REACH) & (jnp.abs(col_k - col_q) <= REACH)
        for row in (row_k, row_q):
            ok = ok & (row + first_row >= 0) & (row + first_row < 8 * lats)
        return jnp.where(ok, 0.0, NEG)

    bias1[...] = bias((SLOTS, 128), 0, 0, 0)
    bias2[...] = bias((128, HALO), 0, 0, NORTH)

    patch = lax.broadcasted_iota(jnp.int32, (128, 128), 0)
    slot = lax.broadcasted_iota(jnp.int32, (128, 128), 1)

    def spread(shift, edge, skip_rows, count):
        t = slot - shift
        r = sixth(jnp.maximum(t, 0))
        want = (r + skip_rows) * 16 + t - 6 * r + edge
        return jnp.where((t >= 0) & (t < count) & (patch == want), 1.0, 0.0).astype(BF16)

    picks[0] = jnp.where(patch == slot + 32, 1.0, 0.0).astype(BF16)
    picks[1] = spread(0, outer_first, 0, 48)
    picks[2] = spread(0, inner_first, 0, 48)
    picks[3] = spread(84, inner_first, 0, 36)
    picks[4] = spread(48, inner_first, 2, 36)

    goes = (has_n, has_s, None, has_n, has_s, None, has_n, has_s)
    comes = (has_s, has_n, None, has_s, has_n, None, has_s, has_n)

    def maybe(cond, f):
        if cond is None:
            f()
        else:
            pl.when(cond)(f)

    def tell(g):
        s = own_stat[g].reshape(16, 128)
        hi = s.astype(BF16)
        rest = s - hi.astype(F32)
        mid = rest.astype(BF16).astype(F32)
        parts = jnp.concatenate((hi.astype(F32), mid, rest - mid), axis=0).astype(BF16)
        send_stat[g, 0] = s
        for i in range(5):
            x = nn(parts, picks[i])
            send_stat[g, i + 1] = x[0:16] + x[16:32] + x[32:48]
        for i in range(8):
            maybe(goes[i], lambda i=i: stat_copy(i, g).start())

    def hear(g):
        for i in range(8):
            maybe(comes[i], lambda i=i: stat_copy(i, g).wait_recv())
        got = recv_stat[g]
        halo_stat[...] = jnp.concatenate(
            (
                got[1][:, :96], got[0][:, :96], got[2][:, :48], got[4][:, :48], got[3][:, :48],
                got[5] + got[6] + got[7],
            ),
            axis=1,
        ).reshape(2, 8, HALO)

    @pl.when(jnp.logical_not(late))
    def _():
        pass_on(lat_copy, 0, (1,))

    outer_copy(0).wait_recv()
    start_both(corner_copy, 0)

    @pl.when(jnp.logical_not(late))
    def _():
        start_both(lat_copy, 1, 0, AHEAD)
        pass_on(lat_copy, 0, (3,))
        each_group(lambda g: rim(0, g))

    @pl.when(holds)
    def _():
        outer_copy(1).start()

    pass_on(corner_copy, 0)


    def arrive(ph, g):
        receive(corner_copy, ph, g)
        inner_copy(ph, g).wait_recv()

    lane = lax.broadcasted_iota(jnp.int32, (128, 128), 1)
    low = jnp.where(lane < HD, 1.0, 0.0).astype(BF16)
    high = jnp.where(lane < HD, 0.0, 1.0).astype(BF16)
    low_f, high_f = low.astype(F32), high.astype(F32)

    def split(x):
        return jnp.concatenate((x * low, x * high), axis=0)

    def joined(x):
        return jnp.concatenate((x[:HD, :128], x[HD:, 128:]), axis=0).T

    def pair_lanes(p):
        return pl.ds(pl.multiple_of(p * 128, 128), 128)

    def first_pass(g, i):
        at = pair_lanes(g * PER + i)
        keys, values = buf[0, :, at], buf[1, :, at]
        queries = split(buf[2, OWN:NORTH, at] * jnp.asarray(0.125, BF16))
        upstream = split(buf[3, OWN:NORTH, at])
        cuts = [(r, min(r + CHUNK, SLOTS)) for r in range(0, SLOTS, CHUNK)]
        peak = jnp.full((8, 256), NEG, F32)
        for lo, hi in cuts:
            near = bias1[lo:hi]
            part = nt(keys[lo:hi], queries) + jnp.concatenate((near, near), axis=1)
            work[lo:hi] = part
            peak = jnp.maximum(peak, jnp.max(part.reshape(-1, 8, 256), axis=0))
        peak = jnp.max(peak, axis=0, keepdims=True)
        total = jnp.zeros((8, 256), F32)
        delta = jnp.zeros((8, 256), F32)
        for lo, hi in cuts:
            e = jnp.exp(work[lo:hi] - peak)
            part = nt(values[lo:hi], upstream)
            work[lo:hi] = e
            work2[lo:hi] = part
            total = total + jnp.sum(e.reshape(-1, 8, 256), axis=0)
            delta = delta + jnp.sum((e * part).reshape(-1, 8, 256), axis=0)
        total = jnp.sum(total, axis=0, keepdims=True)
        scale = 1.0 / total
        delta = jnp.sum(delta, axis=0, keepdims=True) * scale
        for lo, hi in cuts:
            probs = work[lo:hi] * scale
            low_probs[lo:hi] = probs.astype(BF16)
            low_grads[lo:hi] = (probs * (work2[lo:hi] - delta)).astype(BF16)
        probs_low, score_grad = low_probs[...], low_grads[...]
        att[:, at] = joined(tn(values, probs_low)).astype(BF16)
        dq[:, at] = (joined(tn(keys, score_grad)) * 0.125).astype(BF16)
        dv_own[:, at] = nn(probs_low[OWN:NORTH], upstream)
        dk_own[:, at] = nn(score_grad[OWN:NORTH], queries)
        log_total = peak + jnp.log(total)
        for h in range(2):
            here = slice(128 * h, 128 * h + 128)
            own_stat[g // 2, g % 2, 2 * i + h : 2 * i + h + 1, :] = log_total[:, here]
            own_stat[g // 2, g % 2, 4 + 2 * i + h : 5 + 2 * i + h, :] = delta[:, here]

    def second_pass(g, i):
        at = pair_lanes(g * PER + i)
        keys = split(buf[0, OWN:NORTH, at] * jnp.asarray(0.125, BF16))
        values = split(buf[1, OWN:NORTH, at])
        queries, upstream = buf[2, NORTH:SLOTS, at], buf[3, NORTH:SLOTS, at]
        scores = nt(keys, queries)
        prob_grad = nt(values, upstream)
        near = bias2[...]
        lows, grads = [], []
        for h in range(2):
            here = slice(128 * h, 128 * h + 128)
            probs = jnp.exp(scores[here] + near - halo_stat[g % 2, 2 * i + h : 2 * i + h + 1, :])
            lows.append(probs.astype(BF16))
            change = prob_grad[here] - halo_stat[g % 2, 4 + 2 * i + h : 5 + 2 * i + h, :]
            grads.append((probs * change).astype(BF16))
        value_part = nn(jnp.concatenate(lows, axis=0), upstream)
        key_part = nn(jnp.concatenate(grads, axis=0), queries)
        value_part = value_part[:128] * low_f + value_part[128:] * high_f
        key_part = key_part[:128] * low_f + key_part[128:] * high_f
        dv[:, at] = (dv_own[:, at] + value_part).astype(BF16)
        dk[:, at] = (dk_own[:, at] + key_part * 0.125).astype(BF16)

    def pairs_of(g, f):
        for i in range(PER):
            f(g, i)

    def outer_rest():
        outer_copy(1).wait_recv()
        start_both(corner_copy, 1)

    def first_group(g):
        @pl.when(late & (g == 2))
        def _():
            outer_rest()

        arrive(0, g)
        pairs_of(g, first_pass)
        pl.when(g % 2 == 1)(lambda: tell(g // 2))

        @pl.when(jnp.logical_not(late) & (g >= AHEAD - 1) & (g < jnp.where(turn == 7, GROUPS - 2, GROUPS - 1)))
        def _():
            send(lat_copy, True, 1, g + 1)
            send(lat_copy, False, 1, g + 1)

        @pl.when(g == 1)
        def _():
            pass_on(lat_copy, 1, (1,))

    each_group(first_group)

    stores = [
        pltpu.make_async_copy(att, outs.at[0], out_sem.at[0]),
        pltpu.make_async_copy(dq, outs.at[1], out_sem.at[1]),
    ]
    for store in stores:
        store.start()

    @pl.when(turn == 7)
    def _():
        send(lat_copy, True, 1, GROUPS - 1)
        send(lat_copy, False, 1, GROUPS - 1)

    @pl.when(jnp.logical_not(late))
    def _():
        outer_rest()

    pass_on(lat_copy, 1, (3,))
    each_group(lambda g: rim(1, g))
    pass_on(corner_copy, 1)

    def finals(g):
        return [
            pltpu.make_async_copy(
                x.at[:, lanes(g)], outs.at[2 + i, :, lanes(g)], fin_sem.at[i, g]
            )
            for i, x in enumerate((dk, dv))
        ]

    def second_group(g):
        pl.when(g % 2 == 0)(lambda: hear(g // 2))
        arrive(1, g)
        pairs_of(g, second_pass)
        for copy in finals(g):
            copy.start()

    each_group(second_group)

    for ph in range(2):
        for copy in (lat_copy, corner_copy):
            def sent(g):
                wait_sent(copy, True, ph, g)
                wait_sent(copy, False, ph, g)

            each_group(sent)

        outer_copy(ph).wait_send()
        each_group(lambda g: inner_copy(ph, g).wait_send())
    for i in range(8):
        maybe(goes[i], lambda i=i: each_group(lambda g: stat_copy(i, g).wait_send(), 0, TOLD))
    for store in stores:
        store.wait()

    def ended(g):
        for copy in finals(g):
            copy.wait()

    each_group(ended)


def body(lats, lons, queries, keys, values, cotangent):
    flat = [
        pltpu.with_memory_space_constraint(x.reshape(128, 1024), pltpu.HBM)
        for x in (keys, values, queries, cotangent)
    ]
    dma = pltpu.SemaphoreType.DMA
    outs = pl.pallas_call(
        functools.partial(kernel, lats, lons),
        out_shape=jax.ShapeDtypeStruct((4, 128, 1024), BF16),
        in_specs=[pl.BlockSpec(memory_space=pltpu.HBM)] * 4,
        out_specs=pl.BlockSpec(memory_space=pl.ANY),
        scratch_shapes=[
            pltpu.VMEM((4, SLOTS, 1024), BF16),
            pltpu.VMEM((4, 48, 1024), BF16),
            pltpu.VMEM((4, 128, 1024), BF16),
            pltpu.VMEM((SLOTS, 128), F32),
            pltpu.VMEM((128, HALO), F32),
            pltpu.VMEM((TOLD, 2, 8, 128), F32),
            pltpu.VMEM((TOLD, 6, 16, 128), F32),
            pltpu.VMEM((TOLD, 8, 16, 128), F32),
            pltpu.VMEM((2, 8, HALO), F32),
            pltpu.VMEM((128, 1024), BF16),
            pltpu.VMEM((128, 1024), BF16),
            pltpu.VMEM((128, 1024), BF16),
            pltpu.VMEM((128, 1024), BF16),
            pltpu.VMEM((128, 1024), F32),
            pltpu.VMEM((128, 1024), F32),
            pltpu.VMEM((SLOTS, 256), F32),
            pltpu.VMEM((SLOTS, 256), F32),
            pltpu.VMEM((SLOTS, 256), BF16),
            pltpu.VMEM((SLOTS, 256), BF16),
            pltpu.VMEM((5, 128, 128), BF16),
            pltpu.SemaphoreType.REGULAR,
            dma((4,)),
            dma((2,)),
            dma((2, GROUPS)),
            dma((2, 2, GROUPS)),
            dma((2, 2, GROUPS)),
            dma((2,)),
            dma((2,)),
            dma((2, 2, GROUPS)),
            dma((2, 2, GROUPS)),
            dma((2, GROUPS)),
            dma((2, GROUPS)),
            dma((8, TOLD)),
            dma((8, TOLD)),
        ],
        compiler_params=pltpu.CompilerParams(
            collective_id=0, has_side_effects=True, vmem_limit_bytes=48 << 20
        ),
    )(*flat)
    return tuple(outs[i].reshape(8, 16, 1024) for i in range(4))


def solution(mesh):
    spec = P("lat", "lon", None)
    return jax.shard_map(
        functools.partial(body, mesh.shape["lat"], mesh.shape["lon"]),
        mesh=mesh,
        in_specs=(spec,) * 4,
        out_specs=(spec,) * 4,
        check_vma=False,
    )
```

```python
import functools

import jax
import jax.numpy as jnp
from jax import lax
from jax.experimental import pallas as pl
from jax.experimental.pallas import tpu as pltpu
from jax.sharding import PartitionSpec as P

HD = 64
REACH = 6
MESH = pl.DeviceIdType.MESH
BF16 = jnp.bfloat16
F32 = jnp.float32

OWN, NORTH, SOUTH, OUTER, OUTER_N, OUTER_S, INNER, SLOTS = 0, 128, 224, 320, 368, 416, 464, 592
SIDE = INNER - OUTER
PADDED = INNER + SIDE
HALO = SLOTS - NORTH
GROUPS = 4
PER = 2
TOLD = 2
AHEAD = 2
NEG = -1e30


def nt(a, b):
    return lax.dot_general(a, b, (((1,), (1,)), ((), ())), preferred_element_type=F32)


def tn(a, b):
    return lax.dot_general(a, b, (((0,), (0,)), ((), ())), preferred_element_type=F32)


def nn(a, b):
    return lax.dot_general(a, b, (((1,), (0,)), ((), ())), preferred_element_type=F32)


def sixth(t):
    return (t * 43) >> 8


def place(slot, outer_col, inner_col):
    far = 1000
    s = slot - OUTER
    six = jnp.where(s < 48, s, jnp.where(s < 96, s - 48, s - 96))
    outer_row = sixth(six)
    outer_row = jnp.where(s < 48, outer_row, jnp.where(s < 96, outer_row - 8, outer_row + 8))
    t = slot - INNER
    u = jnp.where(t < 48, t, jnp.where(t < 84, t - 48, t - 84))
    inner_row = sixth(u)
    inner_row = jnp.where(
        t < 48, inner_row, jnp.where(t < 84, inner_row - REACH, jnp.where(t < 120, inner_row + 8, far))
    )
    wide = slot >> 4
    wide_row = jnp.where(slot < NORTH, wide, jnp.where(slot < SOUTH, wide - 14, wide - 6))
    row = jnp.where(slot < OUTER, wide_row, jnp.where(slot < INNER, outer_row, inner_row))
    col = jnp.where(
        slot < OUTER,
        slot & 15,
        jnp.where(slot < INNER, outer_col + six - 6 * sixth(six), inner_col + u - 6 * sixth(u)),
    )
    return row, col


def kernel(
    lats, lons, k_in, v_in, q_in, g_in, outs,
    buf, osend, isend, bias1, bias2, own_stat, send_stat, recv_stat, halo_stat,
    att, dq, dk, dv, dk_own, dv_own, work, work2, low_probs, low_grads,
    picks, ready, in_sem, out_sem, fin_sem, lat_s, lat_r, out_s, out_r, cor_s, cor_r, inn_s, inn_r, st_s, st_r,
):
    lat, lon = lax.axis_index("lat"), lax.axis_index("lon")
    core = lax.rem(lon, 2)
    has_n, has_s = lat > 0, lat < lats - 1
    half = lats // 2
    far_s, far_n = lat == half - 1, lat == half
    first, last = lat == 0, lat == lats - 1
    meets = far_s | far_n | first | last
    north, south = jnp.maximum(lat - 1, 0), jnp.minimum(lat + 1, lats - 1)
    outer = jnp.where(core == 0, lax.rem(lon + lons - 1, lons), lax.rem(lon + 1, lons))
    inner = jnp.where(core == 0, lon + 1, lon - 1)
    turn = lax.rem(lon, 8)
    late = turn == 0
    asks = late | ((core == 1) & (turn < 7))
    outer_col = jnp.where(core == 0, -REACH, 16)
    inner_col = jnp.where(core == 0, 16, -REACH)
    outer_first = jnp.where(core == 0, 0, 16 - REACH)
    inner_first = jnp.where(core == 0, 16 - REACH, 0)

    loads = [
        pltpu.make_async_copy(x, buf.at[i, OWN:NORTH, :], in_sem.at[i])
        for i, x in enumerate((k_in, v_in, q_in, g_in))
    ]
    for load in loads:
        load.start()

    @pl.when(jnp.logical_not(has_n))
    def _():
        buf[:, NORTH:SOUTH, :] = jnp.zeros((4, SOUTH - NORTH, 1024), BF16)
        buf[:, OUTER_N:OUTER_S, :] = jnp.zeros((4, 48, 1024), BF16)

    @pl.when(jnp.logical_not(has_s))
    def _():
        buf[:, SOUTH:OUTER, :] = jnp.zeros((4, OUTER - SOUTH, 1024), BF16)
        buf[:, OUTER_S:INNER, :] = jnp.zeros((4, 48, 1024), BF16)

    buf[0:2, SLOTS:PADDED, :] = jnp.zeros((2, PADDED - SLOTS, 1024), BF16)
    recv_stat[...] = jnp.zeros(recv_stat.shape, F32)

    barrier = pltpu.get_barrier_semaphore()
    def greet(sem, col, with_row):
        if with_row:
            pl.semaphore_signal(sem, inc=1, device_id={"lon": col}, device_id_type=MESH)

        @pl.when(has_n)
        def _():
            pl.semaphore_signal(
                sem, inc=1, device_id={"lat": north, "lon": col}, device_id_type=MESH
            )

        @pl.when(has_s)
        def _():
            pl.semaphore_signal(
                sem, inc=1, device_id={"lat": south, "lon": col}, device_id_type=MESH
            )

    greet(barrier, lon, False)
    greet(barrier, inner, True)

    @pl.when(asks)
    def _():
        greet(barrier, outer, True)

    for a in (0, 1):
        to = jnp.where(far_s | far_n, (0, lats - 1)[a], half - 1 + a)

        @pl.when(meets)
        def _():
            pl.semaphore_signal(barrier, inc=1, device_id={"lat": to}, device_id_type=MESH)

    rows = jnp.where(has_n, 1, 0) + jnp.where(has_s, 1, 0)
    pl.semaphore_wait(
        barrier,
        2 * rows + 1 + jnp.where(asks, 0, rows + 1) + 2 * jnp.where(meets, 1, 0),
    )

    @pl.when(jnp.logical_not(asks))
    def _():
        greet(ready, outer, True)

    for load in loads:
        load.wait()

    width = 1024 // GROUPS

    def lanes(g):
        return pl.ds(pl.multiple_of(g * width, width), width)

    def lat_move(sends, recvs, src, dst, ph, g, to_north, lands_north, to):
        rows = 96 if sends is lat_s else 48
        return pltpu.make_async_remote_copy(
            buf.at[2 * ph : 2 * ph + 2, src : src + rows, lanes(g)],
            buf.at[2 * ph : 2 * ph + 2, dst : dst + rows, lanes(g)],
            sends.at[0 if to_north else 1, ph, g],
            recvs.at[1 if lands_north else 0, ph, g],
            device_id={"lat": to},
            device_id_type=MESH,
        )

    def lat_copy(to_north, ph, g, way="direct"):
        own = OWN if to_north else OWN + 32
        above, below = NORTH, SOUTH
        return by_way(lat_s, lat_r, own, above, below, to_north, ph, g, way)

    def corner_copy(to_north, ph, g, way="direct"):
        return by_way(cor_s, cor_r, OUTER, OUTER_N, OUTER_S, to_north, ph, g, way)

    def by_way(sends, recvs, own, above, below, to_north, ph, g, way):
        if way == "direct":
            to = north if to_north else south
            return lat_move(
                sends, recvs, own, below if to_north else above, ph, g, to_north, not to_north, to
            )
        if way == "detour":
            to = 0 if to_north else lats - 1
            return lat_move(
                sends, recvs, own, above if to_north else below, ph, g, to_north, to_north, to
            )
        to = half - 1 if to_north else half
        src, dst = (above, below) if to_north else (below, above)
        return lat_move(sends, recvs, src, dst, ph, g, to_north, not to_north, to)

    def send(copy, to_north, ph, g):
        has = has_n if to_north else has_s
        detour = (far_n if to_north else far_s) & (g % 2 == 1)

        @pl.when(has & jnp.logical_not(detour))
        def _():
            copy(to_north, ph, g).start()

        @pl.when(detour)
        def _():
            copy(to_north, ph, g, "detour").start()

    def wait_sent(copy, to_north, ph, g):
        @pl.when((has_n | (g % 2 == 1)) if to_north else (has_s | (g % 2 == 1)))
        def _():
            copy(to_north, ph, g).wait_send()

    def receive(copy, ph, g):
        @pl.when(has_s)
        def _():
            copy(True, ph, g).wait_recv()

        @pl.when(has_n)
        def _():
            copy(False, ph, g).wait_recv()

    def pass_on(copy, ph, groups=range(1, GROUPS, 2)):
        for g in groups:
            @pl.when(first)
            def _():
                copy(False, ph, g).wait_recv()
                copy(True, ph, g, "onward").start()

            @pl.when(last)
            def _():
                copy(True, ph, g).wait_recv()
                copy(False, ph, g, "onward").start()

    def outer_copy(ph):
        return pltpu.make_async_remote_copy(
            osend.at[2 * ph : 2 * ph + 2],
            buf.at[2 * ph : 2 * ph + 2, OUTER : OUTER + 48, :],
            out_s.at[ph],
            out_r.at[ph],
            device_id={"lon": outer},
            device_id_type=MESH,
        )

    def inner_copy(ph, g):
        return pltpu.make_async_remote_copy(
            isend.at[2 * ph : 2 * ph + 2, :, lanes(g)],
            buf.at[2 * ph : 2 * ph + 2, INNER:SLOTS, lanes(g)],
            inn_s.at[ph, g],
            inn_r.at[ph, g],
            device_id={"lon": inner},
            device_id_type=MESH,
        )

    def stat_copy(i, g):
        lat_to, lon_to, part = (
            (north, lon, 0), (south, lon, 1),
            (lat, outer, 2), (north, outer, 2), (south, outer, 2),
            (lat, inner, 3), (north, inner, 4), (south, inner, 5),
        )[i]
        return pltpu.make_async_remote_copy(
            send_stat.at[g, part],
            recv_stat.at[g, i],
            st_s.at[i, g],
            st_r.at[i, g],
            device_id={"lat": lat_to, "lon": lon_to},
            device_id_type=MESH,
        )

    def each_group(f, start=0, stop=GROUPS):
        def step(g, carry):
            f(g)
            return carry

        lax.fori_loop(start, stop, step, 0)

    def start_both(copy, ph, start=0, stop=GROUPS):
        def one(g):
            send(copy, True, ph, g)
            send(copy, False, ph, g)

        each_group(one, start, stop)

    start_both(lat_copy, 0)

    @pl.when(late)
    def _():
        start_both(lat_copy, 1)

    slot = lax.broadcasted_iota(jnp.int32, (48, 128), 0)
    patch = lax.broadcasted_iota(jnp.int32, (48, 128), 1)
    row6 = sixth(slot)
    at = row6 * 16 + slot - 6 * row6
    pick_outer = jnp.where(patch == at + outer_first, 1.0, 0.0).astype(BF16)
    pick_inner = jnp.where(patch == at + inner_first, 1.0, 0.0).astype(BF16)
    slot = lax.broadcasted_iota(jnp.int32, (80, 192), 0)
    patch = lax.broadcasted_iota(jnp.int32, (80, 192), 1)
    row6 = sixth(slot)
    at = row6 * 16 + slot - 6 * row6
    pick_rim = jnp.where((patch == at + inner_first) & (slot < 72), 1.0, 0.0).astype(BF16)

    def rim(ph, g):
        receive(lat_copy, ph, g)
        for i in (2 * ph, 2 * ph + 1):
            isend[i, 48:128, lanes(g)] = nn(pick_rim, buf[i, NORTH:OUTER, lanes(g)]).astype(BF16)
        inner_copy(ph, g).start()

    for i in range(4):
        osend[i] = nn(pick_outer, buf[i, OWN:NORTH, :]).astype(BF16)
        isend[i, 0:48, :] = nn(pick_inner, buf[i, OWN:NORTH, :]).astype(BF16)

    @pl.when(late)
    def _():
        pass_on(lat_copy, 0)
        each_group(lambda g: rim(0, g))

    @pl.when(asks)
    def _():
        pl.semaphore_wait(ready, rows + 1)

    outer_copy(0).start()
    holds = turn != 7

    @pl.when(jnp.logical_not(holds))
    def _():
        outer_copy(1).start()

    first_row = lat * 8

    def bias(shape, key_axis, first_key, first_query):
        row_k, col_k = place(
            lax.broadcasted_iota(jnp.int32, shape, key_axis) + first_key, outer_col, inner_col
        )
        row_q, col_q = place(
            lax.broadcasted_iota(jnp.int32, shape, 1 - key_axis) + first_query, outer_col, inner_col
        )
        ok = (jnp.abs(row_k - row_q) <= REACH) & (jnp.abs(col_k - col_q) <= REACH)
        for row in (row_k, row_q):
            ok = ok & (row + first_row >= 0) & (row + first_row < 8 * lats)
        return jnp.where(ok, 0.0, NEG)

    bias1[0:OUTER] = bias((OUTER, 128), 0, 0, 0)
    bias1[OUTER:INNER] = jnp.maximum(
        bias((SIDE, 128), 0, OUTER, 0), bias((SIDE, 128), 0, INNER, 0)
    )
    bias2[...] = bias((128, HALO), 0, 0, NORTH)

    patch = lax.broadcasted_iota(jnp.int32, (128, 128), 0)
    slot = lax.broadcasted_iota(jnp.int32, (128, 128), 1)

    def spread(shift, edge, skip_rows, count):
        t = slot - shift
        r = sixth(jnp.maximum(t, 0))
        want = (r + skip_rows) * 16 + t - 6 * r + edge
        return jnp.where((t >= 0) & (t < count) & (patch == want), 1.0, 0.0).astype(BF16)

    picks[0] = jnp.where(patch == slot + 32, 1.0, 0.0).astype(BF16)
    picks[1] = spread(0, outer_first, 0, 48)
    picks[2] = spread(0, inner_first, 0, 48)
    picks[3] = spread(84, inner_first, 0, 36)
    picks[4] = spread(48, inner_first, 2, 36)

    goes = (has_n, has_s, None, has_n, has_s, None, has_n, has_s)
    comes = (has_s, has_n, None, has_s, has_n, None, has_s, has_n)

    def maybe(cond, f):
        if cond is None:
            f()
        else:
            pl.when(cond)(f)

    def tell(g):
        s = own_stat[g].reshape(16, 128)
        hi = s.astype(BF16)
        rest = s - hi.astype(F32)
        mid = rest.astype(BF16).astype(F32)
        parts = jnp.concatenate((hi.astype(F32), mid, rest - mid), axis=0).astype(BF16)
        send_stat[g, 0] = s
        for i in range(5):
            x = nn(parts, picks[i])
            send_stat[g, i + 1] = x[0:16] + x[16:32] + x[32:48]
        for i in range(8):
            maybe(goes[i], lambda i=i: stat_copy(i, g).start())

    def hear(g):
        for i in range(8):
            maybe(comes[i], lambda i=i: stat_copy(i, g).wait_recv())
        got = recv_stat[g]
        halo_stat[...] = jnp.concatenate(
            (
                got[1][:, :96], got[0][:, :96], got[2][:, :48], got[4][:, :48], got[3][:, :48],
                got[5] + got[6] + got[7],
            ),
            axis=1,
        ).reshape(2, 8, HALO)

    @pl.when(jnp.logical_not(late))
    def _():
        pass_on(lat_copy, 0, (1,))

    outer_copy(0).wait_recv()
    start_both(corner_copy, 0)

    @pl.when(jnp.logical_not(late))
    def _():
        start_both(lat_copy, 1, 0, AHEAD)
        pass_on(lat_copy, 0, (3,))
        each_group(lambda g: rim(0, g))

    @pl.when(holds)
    def _():
        outer_copy(1).start()

    pass_on(corner_copy, 0)


    def arrive(ph, g):
        receive(corner_copy, ph, g)
        inner_copy(ph, g).wait_recv()

    lane = lax.broadcasted_iota(jnp.int32, (128, 128), 1)
    low = jnp.where(lane < HD, 1.0, 0.0).astype(BF16)
    high = jnp.where(lane < HD, 0.0, 1.0).astype(BF16)
    low_f, high_f = low.astype(F32), high.astype(F32)

    def column_mask(shape, axis, edge):
        col = lax.broadcasted_iota(jnp.int32, shape, axis) & 15
        return jnp.where((col >= edge) & (col < edge + REACH), 1.0, 0.0).astype(BF16)

    near_outer = column_mask((256, 128), 0, outer_first)
    near_inner = column_mask((256, 128), 0, inner_first)
    lanes_outer = column_mask((SIDE, 256), 1, outer_first)
    lanes_inner = column_mask((SIDE, 256), 1, inner_first)

    def split(x):
        return jnp.concatenate((x * low, x * high), axis=0)

    def joined(x):
        return jnp.concatenate((x[:HD, :128], x[HD:, 128:]), axis=0).T

    def pair_lanes(p):
        return pl.ds(pl.multiple_of(p * 128, 128), 128)

    def first_pass(g, i):
        at = pair_lanes(g * PER + i)
        keys, values = buf[0, :, at], buf[1, :, at]
        queries = split(buf[2, OWN:NORTH, at] * jnp.asarray(0.125, BF16))
        upstream = split(buf[3, OWN:NORTH, at])

        def product(x, lo, hi, y):
            if lo < OUTER:
                return nt(x[lo:hi], y)
            both = jnp.concatenate((x[OUTER:INNER], x[INNER:PADDED]), axis=1)
            return nt(both, jnp.concatenate((y * near_outer, y * near_inner), axis=1))

        cuts = [(0, 160), (160, OUTER), (OUTER, INNER)]
        peak = jnp.full((8, 256), NEG, F32)
        for lo, hi in cuts:
            near = bias1[lo:hi]
            part = product(keys, lo, hi, queries) + jnp.concatenate((near, near), axis=1)
            work[lo:hi] = part
            peak = jnp.maximum(peak, jnp.max(part.reshape(-1, 8, 256), axis=0))
        peak = jnp.max(peak, axis=0, keepdims=True)
        total = jnp.zeros((8, 256), F32)
        delta = jnp.zeros((8, 256), F32)
        for lo, hi in cuts:
            e = jnp.exp(work[lo:hi] - peak)
            part = product(values, lo, hi, upstream)
            work[lo:hi] = e
            work2[lo:hi] = part
            total = total + jnp.sum(e.reshape(-1, 8, 256), axis=0)
            delta = delta + jnp.sum((e * part).reshape(-1, 8, 256), axis=0)
        total = jnp.sum(total, axis=0, keepdims=True)
        scale = 1.0 / total
        delta = jnp.sum(delta, axis=0, keepdims=True) * scale
        for lo, hi in cuts:
            probs = work[lo:hi] * scale
            probs_bf = probs.astype(BF16)
            grads_bf = (probs * (work2[lo:hi] - delta)).astype(BF16)
            if lo < OUTER:
                low_probs[lo:hi] = probs_bf
                low_grads[lo:hi] = grads_bf
            else:
                low_probs[lo:hi] = probs_bf * lanes_outer
                low_grads[lo:hi] = grads_bf * lanes_outer
                low_probs[INNER:PADDED] = probs_bf * lanes_inner
                low_grads[INNER:PADDED] = grads_bf * lanes_inner
        probs_low, score_grad = low_probs[...], low_grads[...]
        att[:, at] = joined(tn(values, probs_low)).astype(BF16)
        dq[:, at] = (joined(tn(keys, score_grad)) * 0.125).astype(BF16)
        dv_own[:, at] = nn(probs_low[OWN:NORTH], upstream)
        dk_own[:, at] = nn(score_grad[OWN:NORTH], queries)
        log_total = peak + jnp.log(total)
        for h in range(2):
            here = slice(128 * h, 128 * h + 128)
            own_stat[g // 2, g % 2, 2 * i + h : 2 * i + h + 1, :] = log_total[:, here]
            own_stat[g // 2, g % 2, 4 + 2 * i + h : 5 + 2 * i + h, :] = delta[:, here]

    def second_pass(g, i):
        at = pair_lanes(g * PER + i)
        keys = split(buf[0, OWN:NORTH, at] * jnp.asarray(0.125, BF16))
        values = split(buf[1, OWN:NORTH, at])
        queries, upstream = buf[2, NORTH:SLOTS, at], buf[3, NORTH:SLOTS, at]
        scores = nt(keys, queries)
        prob_grad = nt(values, upstream)
        near = bias2[...]
        lows, grads = [], []
        for h in range(2):
            here = slice(128 * h, 128 * h + 128)
            probs = jnp.exp(scores[here] + near - halo_stat[g % 2, 2 * i + h : 2 * i + h + 1, :])
            lows.append(probs.astype(BF16))
            change = prob_grad[here] - halo_stat[g % 2, 4 + 2 * i + h : 5 + 2 * i + h, :]
            grads.append((probs * change).astype(BF16))
        value_part = nn(jnp.concatenate(lows, axis=0), upstream)
        key_part = nn(jnp.concatenate(grads, axis=0), queries)
        value_part = value_part[:128] * low_f + value_part[128:] * high_f
        key_part = key_part[:128] * low_f + key_part[128:] * high_f
        dv[:, at] = (dv_own[:, at] + value_part).astype(BF16)
        dk[:, at] = (dk_own[:, at] + key_part * 0.125).astype(BF16)

    def pairs_of(g, f):
        for i in range(PER):
            f(g, i)

    def outer_rest():
        outer_copy(1).wait_recv()
        start_both(corner_copy, 1)

    def first_group(g):
        @pl.when(late & (g == 2))
        def _():
            outer_rest()

        arrive(0, g)
        pairs_of(g, first_pass)
        pl.when(g % 2 == 1)(lambda: tell(g // 2))

        @pl.when(jnp.logical_not(late) & (g >= AHEAD - 1) & (g < jnp.where(turn == 7, GROUPS - 2, GROUPS - 1)))
        def _():
            send(lat_copy, True, 1, g + 1)
            send(lat_copy, False, 1, g + 1)

        @pl.when(g == 1)
        def _():
            pass_on(lat_copy, 1, (1,))

    each_group(first_group)

    stores = [
        pltpu.make_async_copy(att, outs.at[0], out_sem.at[0]),
        pltpu.make_async_copy(dq, outs.at[1], out_sem.at[1]),
    ]
    for store in stores:
        store.start()

    @pl.when(turn == 7)
    def _():
        send(lat_copy, True, 1, GROUPS - 1)
        send(lat_copy, False, 1, GROUPS - 1)

    @pl.when(jnp.logical_not(late))
    def _():
        outer_rest()

    pass_on(lat_copy, 1, (3,))
    each_group(lambda g: rim(1, g))
    pass_on(corner_copy, 1)

    def finals(g):
        return [
            pltpu.make_async_copy(
                x.at[:, lanes(g)], outs.at[2 + i, :, lanes(g)], fin_sem.at[i, g]
            )
            for i, x in enumerate((dk, dv))
        ]

    def second_group(g):
        pl.when(g % 2 == 0)(lambda: hear(g // 2))
        arrive(1, g)
        pairs_of(g, second_pass)
        for copy in finals(g):
            copy.start()

    each_group(second_group)

    for ph in range(2):
        for copy in (lat_copy, corner_copy):
            def sent(g):
                wait_sent(copy, True, ph, g)
                wait_sent(copy, False, ph, g)

            each_group(sent)

        outer_copy(ph).wait_send()
        each_group(lambda g: inner_copy(ph, g).wait_send())
    for i in range(8):
        maybe(goes[i], lambda i=i: each_group(lambda g: stat_copy(i, g).wait_send(), 0, TOLD))
    for store in stores:
        store.wait()

    def ended(g):
        for copy in finals(g):
            copy.wait()

    each_group(ended)


def body(lats, lons, queries, keys, values, cotangent):
    flat = [
        pltpu.with_memory_space_constraint(x.reshape(128, 1024), pltpu.HBM)
        for x in (keys, values, queries, cotangent)
    ]
    dma = pltpu.SemaphoreType.DMA
    outs = pl.pallas_call(
        functools.partial(kernel, lats, lons),
        out_shape=jax.ShapeDtypeStruct((4, 128, 1024), BF16),
        in_specs=[pl.BlockSpec(memory_space=pltpu.HBM)] * 4,
        out_specs=pl.BlockSpec(memory_space=pl.ANY),
        scratch_shapes=[
            pltpu.VMEM((4, PADDED, 1024), BF16),
            pltpu.VMEM((4, 48, 1024), BF16),
            pltpu.VMEM((4, 128, 1024), BF16),
            pltpu.VMEM((INNER, 128), F32),
            pltpu.VMEM((128, HALO), F32),
            pltpu.VMEM((TOLD, 2, 8, 128), F32),
            pltpu.VMEM((TOLD, 6, 16, 128), F32),
            pltpu.VMEM((TOLD, 8, 16, 128), F32),
            pltpu.VMEM((2, 8, HALO), F32),
            pltpu.VMEM((128, 1024), BF16),
            pltpu.VMEM((128, 1024), BF16),
            pltpu.VMEM((128, 1024), BF16),
            pltpu.VMEM((128, 1024), BF16),
            pltpu.VMEM((128, 1024), F32),
            pltpu.VMEM((128, 1024), F32),
            pltpu.VMEM((INNER, 256), F32),
            pltpu.VMEM((INNER, 256), F32),
            pltpu.VMEM((PADDED, 256), BF16),
            pltpu.VMEM((PADDED, 256), BF16),
            pltpu.VMEM((5, 128, 128), BF16),
            pltpu.SemaphoreType.REGULAR,
            dma((4,)),
            dma((2,)),
            dma((2, GROUPS)),
            dma((2, 2, GROUPS)),
            dma((2, 2, GROUPS)),
            dma((2,)),
            dma((2,)),
            dma((2, 2, GROUPS)),
            dma((2, 2, GROUPS)),
            dma((2, GROUPS)),
            dma((2, GROUPS)),
            dma((8, TOLD)),
            dma((8, TOLD)),
        ],
        compiler_params=pltpu.CompilerParams(
            collective_id=0, has_side_effects=True, vmem_limit_bytes=48 << 20
        ),
    )(*flat)
    return tuple(outs[i].reshape(8, 16, 1024) for i in range(4))


def solution(mesh):
    spec = P("lat", "lon", None)
    return jax.shard_map(
        functools.partial(body, mesh.shape["lat"], mesh.shape["lon"]),
        mesh=mesh,
        in_specs=(spec,) * 4,
        out_specs=(spec,) * 4,
        check_vma=False,
    )
```
